768 devices in a mesh: sx: 12 (over z_lo, x), sy: 32 (over z_hi, y), hb: 2 (over core).
Axes of the slice: x: 4, y: 8, z: 12 (z_hi: 4, z_lo: 3; z = z_hi * 3 + z_lo), core: 2. Of those that a mesh axis runs over, the one named last changes fastest.
Arguments:
- state: float32 [6, 5, 48, 256, 256], P('hb', None, 'sx', 'sy'), may hold values from -6 to 6
- forcing: float32 [6, 5, 48, 256, 256], P('hb', None, 'sx', 'sy'), may hold values from -6 to 6
- coef: float32 [48, 256, 256], P('sx', 'sy'), may hold values from 0.3 to 3
- mixing: float32 [5, 5], replicated, may hold values from -2.5 to 2.5
- agglomerate: int32 [48, 256, 256], P('sx', 'sy'), may hold values from 0 to 32767, as said below
Outputs:
- corrected: float32 [6, 5, 48, 256, 256], P('hb', None, 'sx', 'sy')
- residual: float32 [6, 5, 48, 256, 256], P('hb', None, 'sx', 'sy')
The draws below stay inside these ranges and needn't reach their ends.
Inputs may be any that keep to these rules, and one draw needn't show every extreme that they name: `agglomerate`: A fine cell at global position (x, y, z) lies in coarse cell ((x mod 4) // 2, b, z // 2) of its group, with b = y // 2 where x is even, and otherwise b one of (y-1)//2, y//2, (y+1)//2 clipped to 0 .. 127; so every coarse cell holds four or more fine cells.
All inputs are finite; a program needn't handle non-finite values.
Results may differ from the reference program's by a relative error of at most 0.0001.
Values sent between devices are 32-bit elements; how exact they have to be, the bound alone decides.
No kernel may reach another device: no remote copies, remote signals or barrier semaphores. Data moves between devices by JAX's collectives and lax.ppermute only.
A program may use at most 128 MiB of HBM per device.

```python
import math
import jax
import jax.numpy as jnp
from jax import lax

INST = 6
VARS = 5
CX = 4
NX = 48
NY = 256
NZ = 256
CCY = 128
CCZ = 128
CCELLS = 32768
N_SX = 12


def draw_agglomerate(key, part):
    xpos = jnp.arange(NX, dtype=jnp.int32)[:, None, None]
    ypos = jnp.arange(NY, dtype=jnp.int32)[None, :, None]
    zpos = jnp.arange(NZ, dtype=jnp.int32)[None, None, :]
    moved = jax.random.randint(key, (NX, NY, NZ), -1, 2)
    moved = jnp.where(xpos % 2 == 0, 0, moved)
    rowc = jnp.clip((ypos + moved) // 2, 0, CCY - 1)
    colx = xpos % CX // 2
    return ((colx * CCY + rowc) * CCZ + zpos // 2).astype(jnp.int32)


def block_levels(key, extent, split, smallest, largest):
    level = 1.0
    for position, parts in split:
        draws = jax.random.uniform(jax.random.fold_in(jax.random.fold_in(key, 6), position), (parts,), jnp.float32, smallest / len(split), largest / len(split))
        level = level * jnp.repeat(jnp.exp(draws), extent[position] // parts).reshape((-1,) + (1,) * (len(extent) - 1 - position))
    return level


def noise(rng, shape, deviation, limit, cuts=(), held_as=jnp.bfloat16):
    entries = deviation * jax.random.normal(rng, shape, jnp.float32)
    if cuts:
        entries = entries * block_levels(rng, shape, cuts, -0.22, 0.18)
    return jnp.clip(entries, -limit, limit).astype(held_as)


def setup_inputs(seed: int = 0) -> dict:
    streams_of = jax.random.split(jax.random.key(seed), 6)
    state = noise(streams_of[0], (INST, VARS, NX, NY, NZ), 1.0, 6.0, ((0, 2), (2, 12), (3, 32)), jnp.float32)
    forcing = noise(streams_of[1], (INST, VARS, NX, NY, NZ), 1.0, 6.0, ((0, 2), (2, 12), (3, 32)), jnp.float32)
    coef = jnp.clip(jnp.exp(math.log(3.0) - 2.3025851 * jax.random.uniform(streams_of[2], (NX, NY, NZ), jnp.float32) ** block_levels(streams_of[2], (NX, NY, NZ), ((0, 12), (1, 32)), -0.2, 0.2)), 0.3, 3.0)
    mixing = noise(streams_of[3], (VARS, VARS), VARS ** -0.5, 2.5, (), jnp.float32)
    agglomerate = draw_agglomerate(jax.random.fold_in(streams_of[5], 71), 0)
    return {"state": state, "forcing": forcing, "coef": coef, "mixing": mixing, "agglomerate": agglomerate}


def spectral_matrix():
    rows = jnp.arange(INST)[:, None]
    cols = jnp.arange(INST)[None, :]
    diff = rows - cols
    same = diff == 0
    angle = jnp.where(same, 1.0, math.pi * diff.astype(jnp.float32) / INST)
    signs = jnp.where(diff % 2 == 0, 1.0, -1.0)
    return jnp.where(same, 0.0, 0.5 * signs * jnp.cos(angle) / jnp.sin(angle)).astype(jnp.float32)


def operator(field, cell_coef, mixing, spectral):
    padded = jnp.pad(field, ((0, 0), (0, 0), (1, 1), (1, 1), (1, 1)))
    beside = padded[:, :, 2:, 1:-1, 1:-1] + padded[:, :, :-2, 1:-1, 1:-1]
    beside = beside + padded[:, :, 1:-1, 2:, 1:-1] + padded[:, :, 1:-1, :-2, 1:-1]
    beside = beside + padded[:, :, 1:-1, 1:-1, 2:] + padded[:, :, 1:-1, 1:-1, :-2]
    mixed = jnp.einsum("vw,iwxyz->ivxyz", mixing, field, precision=lax.Precision.HIGHEST)
    timed = jnp.einsum("ij,jvxyz->ivxyz", spectral, field, precision=lax.Precision.HIGHEST)
    return cell_coef * (6.0 * field - beside) + mixed + timed + jnp.tanh(field)


def reference(state, forcing, coef, mixing, agglomerate):
    spectral = spectral_matrix()
    residual = forcing - operator(state, coef, mixing, spectral)
    cells = NX * NY * NZ
    total = N_SX * CCELLS
    xpos = jnp.arange(NX, dtype=jnp.int32)[:, None, None]
    target_ids = ((xpos // CX) * CCELLS + agglomerate).reshape(-1).astype(jnp.int32)

    def restrict(values):
        flat = values.reshape(-1, cells).T
        return jax.ops.segment_sum(flat, target_ids, num_segments=total).T

    coarse_shape = (NX // 2, NY // 2, NZ // 2)
    res_c = restrict(residual).reshape((INST, VARS) + coarse_shape)
    sum_c = restrict(state).reshape((INST, VARS) + coarse_shape)
    coef_sum = restrict(coef[None]).reshape(coarse_shape)
    count = restrict(jnp.ones((1, NX, NY, NZ), jnp.float32)).reshape(coarse_shape)
    start = sum_c / count
    coef_c = coef_sum / count
    target = operator(start, coef_c, mixing, spectral) + res_c
    diagonal_term = 6.0 * coef_c + 2.0
    value = start
    for section in range(2):
        value = value + 0.6 * (target - operator(value, coef_c, mixing, spectral)) / diagonal_term
    change = (value - start).reshape(INST, VARS, total)
    corrected = state + change[:, :, target_ids].reshape(state.shape)
    return corrected, residual
```

```python
import functools

import jax
import jax.numpy as jnp
import numpy as np
from jax import lax
from jax.experimental import pallas as pl
from jax.experimental.pallas import tpu as pltpu
from jax.sharding import PartitionSpec as P

INST = 6
HERE = 3
VARS = 5
FIELDS = HERE * VARS
PLANES = 4
ROWS = 8
NZ = 256
CZ = 128
GROUP = 16
WIN = 2 * GROUP
F32 = jnp.float32
BF16 = jnp.bfloat16


def spectral_matrix():
    rows = np.arange(INST)[:, None]
    cols = np.arange(INST)[None, :]
    diff = rows - cols
    same = diff == 0
    angle = np.where(same, 1.0, np.pi * diff / INST).astype(np.float32)
    signs = np.where(diff % 2 == 0, 1.0, -1.0).astype(np.float32)
    return np.where(same, 0.0, 0.5 * signs * np.cos(angle) / np.sin(angle))


SPECTRAL = spectral_matrix()
OWN = [[float(SPECTRAL[i, j]) for j in range(HERE)] for i in range(HERE)]
OTHER = [[float(SPECTRAL[i, j + HERE]) for j in range(HERE)] for i in range(HERE)]


def tile(field, plane):
    return pl.ds((field * PLANES + plane) * ROWS, ROWS)


def window(plane, field):
    return pl.ds((plane * GROUP + field) * ROWS, ROWS)


def row_of(index):
    return pl.ds(index, WIN, stride=ROWS)


def iota(shape, dim):
    return lax.broadcasted_iota(jnp.int32, shape, dim)


def moved_mask(agg_ref, plane):
    block = agg_ref[pl.ds((2 * plane + 1) * ROWS, ROWS), :]
    own = iota((ROWS, NZ), 0) >> 1
    return (((block >> 7) ^ own) & 1).astype(F32)


def pair_sums(values, ones):
    high = values.astype(BF16)
    low = (values - high.astype(F32)).astype(BF16)
    return jnp.dot(high, ones, preferred_element_type=F32) + jnp.dot(
        low, ones, preferred_element_type=F32
    )


def shift_rows(value, amount):
    return pltpu.roll(value, amount % value.shape[0], 0)


def shift_lanes(value, amount):
    return pltpu.roll(value, amount % value.shape[1], 1)


def edges_kernel(state, x_up, x_down, y_up, y_down, halves):
    for field in range(FIELDS):
        x_up[pl.ds(field * ROWS, ROWS), :] = state[tile(field, PLANES - 1), :]
        x_down[pl.ds(field * ROWS, ROWS), :] = state[tile(field, 0), :]
    count = FIELDS * PLANES
    for half in range(2):
        lanes = pl.ds(half * 128, 128)
        halves[half] = state[:, lanes]
        y_up[:, lanes] = halves[half, pl.ds(ROWS - 1, count, stride=ROWS), :]
        y_down[:, lanes] = halves[half, pl.ds(0, count, stride=ROWS), :]


def split_moved(even, odd, mask, parity, inside):
    moved = odd * mask
    beside = jnp.where(parity, shift_rows(moved, -1), shift_rows(moved, 1))
    return even + (odd - moved) + jnp.where(inside, beside, 0.0), beside


def fill_windows(out, sums, rims, summed, ones):
    summed[pl.ds(0, WIN * ROWS), :] = pair_sums(sums[...], ones)
    first = jnp.concatenate([rims[h, row_of(0), :] for h in range(2)], axis=1)
    last = jnp.concatenate([rims[h, row_of(ROWS - 1), :] for h in range(2)], axis=1)
    rim = pair_sums(jnp.concatenate([first, last], axis=0), ones)
    nothing = jnp.zeros((WIN, CZ), F32)
    out[row_of(0), :] = nothing
    out[row_of(7), :] = nothing
    out[row_of(1), :] = rim[WIN:]
    out[row_of(6), :] = rim[:WIN]
    for b in range(4):
        out[row_of(b + 2), :] = summed[row_of(2 * b), :] + summed[row_of(2 * b + 1), :]


def pair_matrix():
    return (iota((NZ, CZ), 0) >> 1 == iota((NZ, CZ), 1)).astype(BF16)


def inner_kernel(mixing, state, forcing, coef, agg, partial, s_win, sums, rims, summed):
    lane = iota((ROWS, NZ), 1)
    row = iota((ROWS, NZ), 0)
    mix = [[mixing[v, w] for w in range(VARS)] for v in range(VARS)]
    for x in range(PLANES):
        c = coef[pl.ds(x * ROWS, ROWS), :]
        for i in range(HERE):
            values = [state[tile(i * VARS + v, x), :] for v in range(VARS)]
            for v in range(VARS):
                field = i * VARS + v
                here = values[v]
                beside = jnp.where(lane == NZ - 1, 0.0, shift_lanes(here, -1))
                beside = beside + jnp.where(lane == 0, 0.0, shift_lanes(here, 1))
                beside = beside + jnp.where(row == ROWS - 1, 0.0, shift_rows(here, -1))
                beside = beside + jnp.where(row == 0, 0.0, shift_rows(here, 1))
                if x > 0:
                    beside = beside + state[tile(field, x - 1), :]
                if x < PLANES - 1:
                    beside = beside + state[tile(field, x + 1), :]
                total = c * (6.0 * here - beside) + jnp.tanh(here)
                for w in range(VARS):
                    total = total + mix[v][w] * values[w]
                for j in range(HERE):
                    if j != i:
                        total = total + OWN[i][j] * state[tile(j * VARS + v, x), :]
                partial[tile(field, x), :] = forcing[tile(field, x), :] - total
    ones = pair_matrix()
    parity = row % 2 == 1
    inside = (row > 0) & (row < ROWS - 1)
    for p in range(2):
        mask = moved_mask(agg, p)
        for field in range(GROUP):
            if field < FIELDS:
                even, odd = (state[tile(field, 2 * p), :], state[tile(field, 2 * p + 1), :])
            else:
                even = coef[pl.ds(2 * p * ROWS, ROWS), :]
                odd = coef[pl.ds((2 * p + 1) * ROWS, ROWS), :]
            kept, beside = split_moved(even, odd, mask, parity, inside)
            sums[window(p, field), :] = kept
            for half in range(2):
                rims[half, window(p, field), :] = beside[:, half * 128 : (half + 1) * 128]
    fill_windows(s_win, sums, rims, summed, ones)


def damping(coef_sum, count):
    inverse = jnp.where(count > 0.0, 1.0 / jnp.maximum(count, 1.0), 0.0)
    coef_c = coef_sum * inverse
    return inverse, coef_c, 0.6 / (6.0 * coef_c + 2.0)


def outer_kernel(
    partial, x_lo, x_hi, y_lo, y_hi, other, coef, agg, s_win,
    residual, r_win, up, down, sums, rims, summed, edge, scaled, halves, coefs,
):
    row = iota((ROWS, NZ), 0)
    for x in range(PLANES):
        c = coef[pl.ds(x * ROWS, ROWS), :]
        for i in range(HERE):
            for v in range(VARS):
                field = i * VARS + v
                total = partial[tile(field, x), :]
                for j in range(HERE):
                    total = total - OTHER[i][j] * other[tile(j * VARS + v, x), :]
                if x == 0:
                    total = total + c * x_lo[pl.ds(field * ROWS, ROWS), :]
                if x == PLANES - 1:
                    total = total + c * x_hi[pl.ds(field * ROWS, ROWS), :]
                for half in range(2):
                    halves[half, tile(field, x), :] = total[:, half * 128 : (half + 1) * 128]
    count = FIELDS * PLANES
    for half in range(2):
        lanes = pl.ds(half * 128, 128)
        coefs[half] = coef[:, lanes]
        for y, halo in ((0, y_lo), (ROWS - 1, y_hi)):
            c4 = coefs[half, pl.ds(y, PLANES, stride=ROWS), :]
            edge[pl.ds(0, PLANES), :] = c4
            edge[pl.ds(PLANES, PLANES), :] = c4
            c8 = edge[...]
            c60 = jnp.concatenate([c8] * (count // 8) + [c8[: count % 8]], axis=0)
            rows = pl.ds(y, count, stride=ROWS)
            halves[half, rows, :] = halves[half, rows, :] + c60 * halo[:, lanes]
        residual[:, lanes] = halves[half]
    ones = pair_matrix()
    parity = row % 2 == 1
    inside = (row > 0) & (row < ROWS - 1)
    for p in range(2):
        mask = moved_mask(agg, p)
        for field in range(GROUP):
            if field < FIELDS:
                even, odd = (residual[tile(field, 2 * p), :], residual[tile(field, 2 * p + 1), :])
            else:
                even = odd = jnp.ones((ROWS, NZ), F32)
            kept, beside = split_moved(even, odd, mask, parity, inside)
            sums[window(p, field), :] = kept
            for half in range(2):
                rims[half, window(p, field), :] = beside[:, half * 128 : (half + 1) * 128]
    fill_windows(r_win, sums, rims, summed, ones)
    for p in range(2):
        _, _, scale = damping(s_win[window(p, FIELDS), :], r_win[window(p, FIELDS), :])
        for field in range(GROUP):
            scaled[window(p, field), :] = scale * r_win[window(p, field), :]
    for out, ready, edge_row, rim_row in ((up, 4, 5, 6), (down, 3, 2, 1)):
        out[pl.ds(0, WIN), :] = scaled[row_of(ready), :]
        out[pl.ds(WIN, WIN), :] = r_win[row_of(edge_row), :]
        out[pl.ds(2 * WIN, WIN), :] = r_win[row_of(rim_row), :]
        out[pl.ds(3 * WIN, WIN), :] = s_win[row_of(edge_row), :]
        out[pl.ds(4 * WIN, WIN), :] = s_win[row_of(rim_row), :]


def first_kernel(r_in, s_in, lo, hi, r_out, s_out, delta, low_plane, high_plane):
    r_out[...] = r_in[...]
    s_out[...] = s_in[...]
    for msg, edge_row, rim_row in ((lo, 1, 2), (hi, 6, 5)):
        r_out[row_of(edge_row), :] = r_out[row_of(edge_row), :] + msg[pl.ds(WIN, WIN), :]
        r_out[row_of(rim_row), :] = r_out[row_of(rim_row), :] + msg[pl.ds(2 * WIN, WIN), :]
        s_out[row_of(edge_row), :] = s_out[row_of(edge_row), :] + msg[pl.ds(3 * WIN, WIN), :]
        s_out[row_of(rim_row), :] = s_out[row_of(rim_row), :] + msg[pl.ds(4 * WIN, WIN), :]
    for p in range(2):
        _, _, scale = damping(s_out[window(p, FIELDS), :], r_out[window(p, FIELDS), :])
        for field in range(GROUP):
            delta[window(p, field), :] = scale * r_out[window(p, field), :]
    delta[row_of(0), :] = lo[pl.ds(0, WIN), :]
    delta[row_of(7), :] = hi[pl.ds(0, WIN), :]
    half = GROUP * ROWS
    low_plane[...] = delta[pl.ds(0, half), :]
    high_plane[...] = delta[pl.ds(half, half), :]


def second_kernel(mixing, r_win, s_win, delta, partial):
    lane = iota((ROWS, CZ), 1)
    mix = [[mixing[v, w] for w in range(VARS)] for v in range(VARS)]
    for p in range(2):
        inverse, coef_c, scale = damping(s_win[window(p, FIELDS), :], r_win[window(p, FIELDS), :])
        for i in range(HERE):
            values = [delta[window(p, i * VARS + v), :] for v in range(VARS)]
            for v in range(VARS):
                field = i * VARS + v
                here = values[v]
                beside = jnp.where(lane == CZ - 1, 0.0, shift_lanes(here, -1))
                beside = beside + jnp.where(lane == 0, 0.0, shift_lanes(here, 1))
                beside = beside + shift_rows(here, -1) + shift_rows(here, 1)
                beside = beside + delta[window(1 - p, field), :]
                total = coef_c * (6.0 * here - beside)
                start = s_win[window(p, field), :] * inverse
                total = total + (jnp.tanh(start + here) - jnp.tanh(start))
                for w in range(VARS):
                    total = total + mix[v][w] * values[w]
                for j in range(HERE):
                    if j != i:
                        total = total + OWN[i][j] * delta[window(p, j * VARS + v), :]
                partial[window(p, field), :] = here + scale * (r_win[window(p, field), :] - total)
        partial[window(p, FIELDS), :] = coef_c


def final_kernel(partial, x_lo, x_hi, other, state, agg, corrected, change, fine, own, beside):
    for p in range(2):
        coef_c = partial[window(p, FIELDS), :]
        scale = 0.6 / (6.0 * coef_c + 2.0)
        halo = x_lo if p == 0 else x_hi
        for i in range(HERE):
            for v in range(VARS):
                field = i * VARS + v
                total = coef_c * halo[pl.ds(field * ROWS, ROWS), :]
                for j in range(HERE):
                    total = total - OTHER[i][j] * other[window(p, j * VARS + v), :]
                change[window(p, field), :] = partial[window(p, field), :] + scale * total
        change[window(p, FIELDS), :] = jnp.zeros((ROWS, CZ), F32)
    twice = (iota((CZ, NZ), 1) >> 1 == iota((CZ, NZ), 0)).astype(BF16)
    for half in range(2):
        fine[half] = pair_sums(change[...], twice[:, half * 128 : (half + 1) * 128])
    for half in range(2):
        rows = [fine[half, row_of(b + 1), :] for b in range(6)]
        for b in range(4):
            own[half, row_of(2 * b), :] = rows[b + 1]
            own[half, row_of(2 * b + 1), :] = rows[b + 1]
            beside[half, row_of(2 * b), :] = rows[b]
            beside[half, row_of(2 * b + 1), :] = rows[b + 2]
    for p in range(2):
        mask = moved_mask(agg, p)
        for half in range(2):
            lanes = pl.ds(half * 128, 128)
            moved = mask[:, half * 128 : (half + 1) * 128] > 0.0
            for field in range(FIELDS):
                kept = own[half, window(p, field), :]
                went = beside[half, window(p, field), :]
                corrected[tile(field, 2 * p), lanes] = state[tile(field, 2 * p), lanes] + kept
                corrected[tile(field, 2 * p + 1), lanes] = state[
                    tile(field, 2 * p + 1), lanes
                ] + jnp.where(moved, went, kept)


VMEM = pl.BlockSpec(memory_space=pltpu.VMEM)
SMEM = pl.BlockSpec(memory_space=pltpu.SMEM)


def call(kernel, outs, scratch, *args, scalars=0):
    return pl.pallas_call(
        kernel,
        out_shape=[jax.ShapeDtypeStruct(s, F32) for s in outs],
        in_specs=[SMEM] * scalars + [VMEM] * (len(args) - scalars),
        out_specs=[VMEM] * len(outs),
        scratch_shapes=[pltpu.VMEM(s, F32) for s in scratch],
        compiler_params=pltpu.CompilerParams(vmem_limit_bytes=40 * 1024 * 1024),
        name=kernel.__name__,
    )(*args)


def shards(state, forcing, coef, mixing, agglomerate):
    shape = state.shape
    fine = (FIELDS * PLANES * ROWS, NZ)
    wins = (WIN * ROWS, CZ)
    state = state.reshape(fine)
    forcing = forcing.reshape(fine)
    coef = coef.reshape(PLANES * ROWS, NZ)
    agg = agglomerate.reshape(PLANES * ROWS, NZ)

    def pairs(axis):
        up = [(i, i + 1) for i in range(lax.axis_size(axis) - 1)]
        return up, [(j, i) for i, j in up]

    sx_up, sx_down = pairs("sx")
    sy_up, sy_down = pairs("sy")
    swap = [(0, 1), (1, 0)]

    other = lax.ppermute(state, "hb", swap)
    halves = (2, FIELDS * PLANES * ROWS, 128)
    x_face = (FIELDS * ROWS, NZ)
    y_face = (FIELDS * PLANES, NZ)
    x_up, x_down, y_up, y_down = call(edges_kernel, [x_face, x_face, y_face, y_face], [halves], state)
    x_lo = lax.ppermute(x_up, "sx", sx_up)
    x_hi = lax.ppermute(x_down, "sx", sx_down)
    y_lo = lax.ppermute(y_up, "sy", sy_up)
    y_hi = lax.ppermute(y_down, "sy", sy_down)
    rows = (WIN * ROWS, NZ)
    rims = (2, WIN * ROWS, 128)
    partial, s_win = call(
        inner_kernel, [fine, wins], [rows, rims, wins], mixing, state, forcing, coef, agg, scalars=1
    )
    msg = (5 * WIN, CZ)
    residual, r_win, up, down = call(
        outer_kernel,
        [fine, wins, msg, msg],
        [rows, rims, wins, (8, 128), wins, halves, (2, PLANES * ROWS, 128)],
        partial, x_lo, x_hi, y_lo, y_hi, other, coef, agg, s_win,
    )
    lo = lax.ppermute(up, "sy", sy_up)
    hi = lax.ppermute(down, "sy", sy_down)
    plane = (GROUP * ROWS, CZ)
    r_win, s_win, delta, low, high = call(
        first_kernel, [wins, wins, wins, plane, plane], [], r_win, s_win, lo, hi
    )
    other_delta = lax.ppermute(delta, "hb", swap)
    d_lo = lax.ppermute(high, "sx", sx_up)
    d_hi = lax.ppermute(low, "sx", sx_down)
    (step,) = call(second_kernel, [wins], [], mixing, r_win, s_win, delta, scalars=1)
    (corrected,) = call(
        final_kernel,
        [fine],
        [wins, (2,) + wins, (2,) + wins, (2,) + wins],
        step, d_lo, d_hi, other_delta, state, agg,
    )
    return corrected.reshape(shape), residual.reshape(shape)


def solution(mesh):
    whole = P("hb", None, "sx", "sy", None)
    return jax.shard_map(
        shards,
        mesh=mesh,
        in_specs=(whole, whole, P("sx", "sy", None), P(), P("sx", "sy", None)),
        out_specs=(whole, whole),
        check_vma=False,
    )
```

```python
import functools

import jax
import jax.numpy as jnp
import numpy as np
from jax import lax
from jax.experimental import pallas as pl
from jax.experimental.pallas import tpu as pltpu
from jax.sharding import PartitionSpec as P

INST = 6
HERE = 3
VARS = 5
FIELDS = HERE * VARS
PLANES = 4
ROWS = 8
NZ = 256
CZ = 128
GROUP = 16
WIN = 2 * GROUP
F32 = jnp.float32
BF16 = jnp.bfloat16


def spectral_matrix():
    rows = np.arange(INST)[:, None]
    cols = np.arange(INST)[None, :]
    diff = rows - cols
    same = diff == 0
    angle = np.where(same, 1.0, np.pi * diff / INST).astype(np.float32)
    signs = np.where(diff % 2 == 0, 1.0, -1.0).astype(np.float32)
    return np.where(same, 0.0, 0.5 * signs * np.cos(angle) / np.sin(angle))


SPECTRAL = spectral_matrix()
OWN = [[float(SPECTRAL[i, j]) for j in range(HERE)] for i in range(HERE)]
OTHER = [[float(SPECTRAL[i, j + HERE]) for j in range(HERE)] for i in range(HERE)]


def tile(field, plane):
    return pl.ds((field * PLANES + plane) * ROWS, ROWS)


def window(plane, field):
    return pl.ds((plane * GROUP + field) * ROWS, ROWS)


def row_of(index):
    return pl.ds(index, WIN, stride=ROWS)


def iota(shape, dim):
    return lax.broadcasted_iota(jnp.int32, shape, dim)


def moved_mask(agg_ref, plane):
    block = agg_ref[pl.ds((2 * plane + 1) * ROWS, ROWS), :]
    own = iota((ROWS, NZ), 0) >> 1
    return (((block >> 7) ^ own) & 1).astype(F32)


def pair_sums(values, ones):
    high = values.astype(BF16)
    low = (values - high.astype(F32)).astype(BF16)
    return jnp.dot(high, ones, preferred_element_type=F32) + jnp.dot(
        low, ones, preferred_element_type=F32
    )


def shift_rows(value, amount):
    return pltpu.roll(value, amount % value.shape[0], 0)


def shift_lanes(value, amount):
    return pltpu.roll(value, amount % value.shape[1], 1)


def even_index(axis):
    return lax.axis_index(axis) % 2 == 0


def choose(flag, value, other):
    return jnp.where(jnp.full(value.shape, flag.astype(jnp.int32)) > 0, value, other)


def edges_kernel(
    state_in, forcing_in, coef_in, agg_in,
    yb, xb, xa, ya, state, forcing, coef, agg, s_win,
    halves, sums, rims, summed, sems,
):
    pairs = ((state_in, state), (coef_in, coef), (agg_in, agg), (forcing_in, forcing))
    copies = [pltpu.make_async_copy(s, d, sems.at[n]) for n, (s, d) in enumerate(pairs)]
    for copy in copies:
        copy.start()
    for copy in copies[:3]:
        copy.wait()
    even_x, even_y = (even_index("sx"), even_index("sy"))
    for field in range(FIELDS):
        high, low = (state[tile(field, PLANES - 1), :], state[tile(field, 0), :])
        xa[pl.ds(field * ROWS, ROWS), :] = choose(even_x, high, low)
        xb[pl.ds(field * ROWS, ROWS), :] = choose(even_x, low, high)
    count = FIELDS * PLANES
    for half in range(2):
        lanes = pl.ds(half * 128, 128)
        halves[half] = state[:, lanes]
        high = halves[half, pl.ds(ROWS - 1, count, stride=ROWS), :]
        low = halves[half, pl.ds(0, count, stride=ROWS), :]
        ya[pl.ds(0, count), lanes] = choose(even_y, high, low)
        yb[pl.ds(0, count), lanes] = choose(even_y, low, high)
        nothing = jnp.zeros((64 - count, 128), F32)
        ya[pl.ds(count, 64 - count), lanes] = nothing
        yb[pl.ds(count, 64 - count), lanes] = nothing
    restrict(state, lambda x: coef[pl.ds(x * ROWS, ROWS), :], agg, s_win, sums, rims, summed)
    for half, (above, below) in enumerate(((5, 2), (6, 1))):
        lanes = pl.ds(half * 128, 128)
        high, low = (s_win[row_of(above), :], s_win[row_of(below), :])
        ya[pl.ds(64, WIN), lanes] = choose(even_y, high, low)
        yb[pl.ds(64, WIN), lanes] = choose(even_y, low, high)
    copies[3].wait()


def split_moved(even, odd, mask, parity, inside):
    moved = odd * mask
    beside = jnp.where(parity, shift_rows(moved, -1), shift_rows(moved, 1))
    return even + (odd - moved) + jnp.where(inside, beside, 0.0), beside


def fill_windows(out, sums, rims, summed, ones):
    summed[pl.ds(0, WIN * ROWS), :] = pair_sums(sums[...], ones)
    first = jnp.concatenate([rims[h, row_of(0), :] for h in range(2)], axis=1)
    last = jnp.concatenate([rims[h, row_of(ROWS - 1), :] for h in range(2)], axis=1)
    rim = pair_sums(jnp.concatenate([first, last], axis=0), ones)
    nothing = jnp.zeros((WIN, CZ), F32)
    out[row_of(0), :] = nothing
    out[row_of(7), :] = nothing
    out[row_of(1), :] = rim[WIN:]
    out[row_of(6), :] = rim[:WIN]
    for b in range(4):
        out[row_of(b + 2), :] = summed[row_of(2 * b), :] + summed[row_of(2 * b + 1), :]


def restrict(fine, last, agg, out, sums, rims, summed):
    row = iota((ROWS, NZ), 0)
    parity = row % 2 == 1
    inside = (row > 0) & (row < ROWS - 1)
    for p in range(2):
        mask = moved_mask(agg, p)
        for field in range(GROUP):
            if field < FIELDS:
                even, odd = (fine[tile(field, 2 * p), :], fine[tile(field, 2 * p + 1), :])
            else:
                even, odd = (last(2 * p), last(2 * p + 1))
            kept, beside = split_moved(even, odd, mask, parity, inside)
            sums[window(p, field), :] = kept
            for half in range(2):
                rims[half, window(p, field), :] = beside[:, half * 128 : (half + 1) * 128]
    fill_windows(out, sums, rims, summed, pair_matrix())


def pair_matrix():
    return (iota((NZ, CZ), 0) >> 1 == iota((NZ, CZ), 1)).astype(BF16)


def inner_kernel(mixing, state, forcing, coef, partial):
    lane = iota((ROWS, NZ), 1)
    row = iota((ROWS, NZ), 0)
    mix = [[mixing[v, w] for w in range(VARS)] for v in range(VARS)]
    for x in range(PLANES):
        c = coef[pl.ds(x * ROWS, ROWS), :]
        for i in range(HERE):
            values = [state[tile(i * VARS + v, x), :] for v in range(VARS)]
            for v in range(VARS):
                field = i * VARS + v
                here = values[v]
                beside = jnp.where(lane == NZ - 1, 0.0, shift_lanes(here, -1))
                beside = beside + jnp.where(lane == 0, 0.0, shift_lanes(here, 1))
                beside = beside + jnp.where(row == ROWS - 1, 0.0, shift_rows(here, -1))
                beside = beside + jnp.where(row == 0, 0.0, shift_rows(here, 1))
                if x > 0:
                    beside = beside + state[tile(field, x - 1), :]
                if x < PLANES - 1:
                    beside = beside + state[tile(field, x + 1), :]
                total = c * (6.0 * here - beside) + jnp.tanh(here)
                for w in range(VARS):
                    total = total + mix[v][w] * values[w]
                for j in range(HERE):
                    if j != i:
                        total = total + OWN[i][j] * state[tile(j * VARS + v, x), :]
                partial[tile(field, x), :] = forcing[tile(field, x), :] - total


def damping(coef_sum, count):
    inverse = jnp.where(count > 0.0, 1.0 / jnp.maximum(count, 1.0), 0.0)
    coef_c = coef_sum * inverse
    return inverse, coef_c, 0.6 / (6.0 * coef_c + 2.0)


def outer_kernel(
    partial, xa, xb, ya, yb, other, coef, agg, s_in,
    mb, ma, residual, r_win, s_win, sums, rims, summed, edge, scaled, halves, coefs,
):
    even_x, even_y = (even_index("sx"), even_index("sy"))
    for x in range(PLANES):
        c = coef[pl.ds(x * ROWS, ROWS), :]
        for i in range(HERE):
            for v in range(VARS):
                field = i * VARS + v
                face = pl.ds(field * ROWS, ROWS)
                total = partial[tile(field, x), :]
                for j in range(HERE):
                    total = total - OTHER[i][j] * other[tile(j * VARS + v, x), :]
                if x == 0:
                    total = total + c * choose(even_x, xb[face, :], xa[face, :])
                if x == PLANES - 1:
                    total = total + c * choose(even_x, xa[face, :], xb[face, :])
                for half in range(2):
                    halves[half, tile(field, x), :] = total[:, half * 128 : (half + 1) * 128]
    count = FIELDS * PLANES
    for half in range(2):
        lanes = pl.ds(half * 128, 128)
        coefs[half] = coef[:, lanes]
        at_a, at_b = (ya[pl.ds(0, count), lanes], yb[pl.ds(0, count), lanes])
        for y, halo in ((0, choose(even_y, at_b, at_a)), (ROWS - 1, choose(even_y, at_a, at_b))):
            c4 = coefs[half, pl.ds(y, PLANES, stride=ROWS), :]
            edge[pl.ds(0, PLANES), :] = c4
            edge[pl.ds(PLANES, PLANES), :] = c4
            c8 = edge[...]
            c60 = jnp.concatenate([c8] * (count // 8) + [c8[: count % 8]], axis=0)
            rows = pl.ds(y, count, stride=ROWS)
            halves[half, rows, :] = halves[half, rows, :] + c60 * halo
        residual[:, lanes] = halves[half]
    restrict(residual, lambda x: jnp.ones((ROWS, NZ), F32), agg, r_win, sums, rims, summed)
    s_win[...] = s_in[...]
    for half, (above, below) in enumerate(((6, 1), (5, 2))):
        lanes = pl.ds(half * 128, 128)
        at_a, at_b = (ya[pl.ds(64, WIN), lanes], yb[pl.ds(64, WIN), lanes])
        s_win[row_of(below), :] = s_win[row_of(below), :] + choose(even_y, at_b, at_a)
        s_win[row_of(above), :] = s_win[row_of(above), :] + choose(even_y, at_a, at_b)
    for p in range(2):
        _, _, scale = damping(s_win[window(p, FIELDS), :], r_win[window(p, FIELDS), :])
        for field in range(GROUP):
            scaled[window(p, field), :] = scale * r_win[window(p, field), :]
    pieces = ((scaled, 4, 3), (r_win, 5, 2), (r_win, 6, 1))
    for n, (ref, above, below) in enumerate(pieces):
        high, low = (ref[row_of(above), :], ref[row_of(below), :])
        ma[pl.ds(n * WIN, WIN), :] = choose(even_y, high, low)
        mb[pl.ds(n * WIN, WIN), :] = choose(even_y, low, high)


def store_kernel(values, r_in, out, r_out, sems):
    copy = pltpu.make_async_copy(values, out, sems.at[0])
    copy.start()
    r_out[...] = r_in[...]
    copy.wait()


EDGE_ROWS = 6


def first_kernel(r_in, s_win, ma, mb, xb, xa, delta, r_win):
    even_x, even_y = (even_index("sx"), even_index("sy"))
    r_win[...] = r_in[...]
    pieces = []
    for n in range(3):
        at_a, at_b = (ma[pl.ds(n * WIN, WIN), :], mb[pl.ds(n * WIN, WIN), :])
        pieces.append((choose(even_y, at_b, at_a), choose(even_y, at_a, at_b)))
    for n, below, above in ((1, 1, 6), (2, 2, 5)):
        r_win[row_of(below), :] = r_win[row_of(below), :] + pieces[n][0]
        r_win[row_of(above), :] = r_win[row_of(above), :] + pieces[n][1]
    for p in range(2):
        _, _, scale = damping(s_win[window(p, FIELDS), :], r_win[window(p, FIELDS), :])
        for field in range(GROUP):
            delta[window(p, field), :] = scale * r_win[window(p, field), :]
    delta[row_of(0), :] = pieces[0][0]
    delta[row_of(7), :] = pieces[0][1]
    for r in range(EDGE_ROWS):
        low = delta[pl.ds(r + 1, GROUP, stride=ROWS), :]
        high = delta[pl.ds(GROUP * ROWS + r + 1, GROUP, stride=ROWS), :]
        xa[pl.ds(r * GROUP, GROUP), :] = choose(even_x, high, low)
        xb[pl.ds(r * GROUP, GROUP), :] = choose(even_x, low, high)


def second_kernel(mixing, r_win, s_win, delta, partial):
    lane = iota((ROWS, CZ), 1)
    mix = [[mixing[v, w] for w in range(VARS)] for v in range(VARS)]
    for p in range(2):
        inverse, coef_c, scale = damping(s_win[window(p, FIELDS), :], r_win[window(p, FIELDS), :])
        for i in range(HERE):
            values = [delta[window(p, i * VARS + v), :] for v in range(VARS)]
            for v in range(VARS):
                field = i * VARS + v
                here = values[v]
                beside = jnp.where(lane == CZ - 1, 0.0, shift_lanes(here, -1))
                beside = beside + jnp.where(lane == 0, 0.0, shift_lanes(here, 1))
                beside = beside + shift_rows(here, -1) + shift_rows(here, 1)
                beside = beside + delta[window(1 - p, field), :]
                total = coef_c * (6.0 * here - beside)
                start = s_win[window(p, field), :] * inverse
                total = total + (jnp.tanh(start + here) - jnp.tanh(start))
                for w in range(VARS):
                    total = total + mix[v][w] * values[w]
                for j in range(HERE):
                    if j != i:
                        total = total + OWN[i][j] * delta[window(p, j * VARS + v), :]
                partial[window(p, field), :] = here + scale * (r_win[window(p, field), :] - total)
        partial[window(p, FIELDS), :] = coef_c


def final_kernel(
    partial, xa, xb, other, state, agg, corrected, change, fine, own, beside, halos, result, sems
):
    even_x = even_index("sx")
    for r in range(EDGE_ROWS):
        at_a, at_b = (xa[pl.ds(r * GROUP, GROUP), :], xb[pl.ds(r * GROUP, GROUP), :])
        rows = pl.ds(r + 1, GROUP, stride=ROWS)
        halos[0, rows, :] = choose(even_x, at_b, at_a)
        halos[1, rows, :] = choose(even_x, at_a, at_b)
    for p in range(2):
        for r in (0, ROWS - 1):
            halos[p, pl.ds(r, GROUP, stride=ROWS), :] = jnp.zeros((GROUP, CZ), F32)
    for p in range(2):
        coef_c = partial[window(p, FIELDS), :]
        scale = 0.6 / (6.0 * coef_c + 2.0)
        for i in range(HERE):
            for v in range(VARS):
                field = i * VARS + v
                total = coef_c * halos[p, pl.ds(field * ROWS, ROWS), :]
                for j in range(HERE):
                    total = total - OTHER[i][j] * other[window(p, j * VARS + v), :]
                change[window(p, field), :] = partial[window(p, field), :] + scale * total
        change[window(p, FIELDS), :] = jnp.zeros((ROWS, CZ), F32)
    twice = (iota((CZ, NZ), 1) >> 1 == iota((CZ, NZ), 0)).astype(BF16)
    for half in range(2):
        fine[half] = pair_sums(change[...], twice[:, half * 128 : (half + 1) * 128])
    for half in range(2):
        rows = [fine[half, row_of(b + 1), :] for b in range(6)]
        for b in range(4):
            own[half, row_of(2 * b), :] = rows[b + 1]
            own[half, row_of(2 * b + 1), :] = rows[b + 1]
            beside[half, row_of(2 * b), :] = rows[b]
            beside[half, row_of(2 * b + 1), :] = rows[b + 2]
    masks = [moved_mask(agg, p) > 0.0 for p in range(2)]
    copies = []
    for i in range(HERE):
        for field in range(i * VARS, (i + 1) * VARS):
            for p in range(2):
                for half in range(2):
                    lanes = pl.ds(half * 128, 128)
                    moved = masks[p][:, half * 128 : (half + 1) * 128]
                    kept = own[half, window(p, field), :]
                    went = beside[half, window(p, field), :]
                    even, odd = (tile(field, 2 * p), tile(field, 2 * p + 1))
                    result[even, lanes] = state[even, lanes] + kept
                    result[odd, lanes] = state[odd, lanes] + jnp.where(moved, went, kept)
        rows = pl.ds(i * VARS * PLANES * ROWS, VARS * PLANES * ROWS)
        copies.append(pltpu.make_async_copy(result.at[rows, :], corrected.at[rows, :], sems.at[i]))
        copies[-1].start()
    for copy in copies:
        copy.wait()


VMEM = pl.BlockSpec(memory_space=pltpu.VMEM)
SMEM = pl.BlockSpec(memory_space=pltpu.SMEM)
HBM = pl.BlockSpec(memory_space=pltpu.HBM)


def call(kernel, outs, scratch, *args, spaces=(), out_space=VMEM, sems=0):
    spaces = list(spaces) + [VMEM] * (len(args) - len(spaces))
    args = [
        pltpu.with_memory_space_constraint(a, pltpu.HBM) if s is HBM else a
        for a, s in zip(args, spaces)
    ]
    outs = [o if hasattr(o, "dtype") else jax.ShapeDtypeStruct(o, F32) for o in outs]
    return pl.pallas_call(
        kernel,
        out_shape=outs,
        in_specs=spaces,
        out_specs=out_space if isinstance(out_space, list) else [out_space] * len(outs),
        scratch_shapes=[pltpu.VMEM(s, F32) for s in scratch]
        + ([pltpu.SemaphoreType.DMA((sems,))] if sems else []),
        compiler_params=pltpu.CompilerParams(vmem_limit_bytes=40 * 1024 * 1024),
        name=kernel.__name__,
    )(*args)


def swap_pairs(axis, first):
    size = lax.axis_size(axis)
    up = [(i, i + 1) for i in range(first, size - 1, 2)]
    return up + [(j, i) for i, j in up]


def shards(state, forcing, coef, mixing, agglomerate):
    shape = state.shape
    fine = (FIELDS * PLANES * ROWS, NZ)
    wins = (WIN * ROWS, CZ)
    state = state.reshape(fine)
    forcing = forcing.reshape(fine)
    coef = coef.reshape(PLANES * ROWS, NZ)
    agg = agglomerate.reshape(PLANES * ROWS, NZ)

    def swap(value, axis, first=0):
        return lax.ppermute(value, axis, swap_pairs(axis, first))

    halves = (2, FIELDS * PLANES * ROWS, 128)
    sums = (WIN * ROWS, NZ)
    rims = (2, WIN * ROWS, 128)
    x_face = (FIELDS * ROWS, NZ)
    y_face = (64 + WIN, NZ)
    yb, xb, xa, ya, state, forcing, coef, agg, s_win = call(
        edges_kernel,
        [y_face, x_face, x_face, y_face, fine, fine, coef.shape, agg, wins],
        [halves, sums, rims, wins],
        state, forcing, coef, agg,
        spaces=[HBM] * 4,
        sems=4,
    )
    yb = swap(yb, "sy", 1)
    xb = swap(xb, "sx", 1)
    xa = swap(xa, "sx")
    ya = swap(ya, "sy")
    other = swap(state, "hb")
    (partial,) = call(inner_kernel, [fine], [], mixing, state, forcing, coef, spaces=[SMEM])
    msg = (3 * WIN, CZ)
    mb, ma, residual, r_win, s_win = call(
        outer_kernel,
        [msg, msg, fine, wins, wins],
        [sums, rims, wins, (8, 128), wins, halves, (2, PLANES * ROWS, 128)],
        partial, xa, xb, ya, yb, other, coef, agg, s_win,
    )
    mb = swap(mb, "sy", 1)
    ma = swap(ma, "sy")
    residual, r_win = call(
        store_kernel, [fine, wins], [], residual, r_win, out_space=[HBM, VMEM], sems=1
    )
    face = (EDGE_ROWS * GROUP, CZ)
    db, da, delta, r_win = call(
        first_kernel, [face, face, wins, wins], [], r_win, s_win, ma, mb
    )
    db = swap(db, "sx", 1)
    da = swap(da, "sx")
    other_delta = swap(delta, "hb")
    (step,) = call(second_kernel, [wins], [], mixing, r_win, s_win, delta, spaces=[SMEM])
    (corrected,) = call(
        final_kernel,
        [fine],
        [wins, (2,) + wins, (2,) + wins, (2,) + wins, (2, GROUP * ROWS, CZ), fine],
        step, da, db, other_delta, state, agg,
        out_space=HBM,
        sems=HERE,
    )
    return corrected.reshape(shape), residual.reshape(shape)


def solution(mesh):
    whole = P("hb", None, "sx", "sy", None)
    return jax.shard_map(
        shards,
        mesh=mesh,
        in_specs=(whole, whole, P("sx", "sy", None), P(), P("sx", "sy", None)),
        out_specs=(whole, whole),
        check_vma=False,
    )
```

```python
import functools

import jax
import jax.numpy as jnp
import numpy as np
from jax import lax
from jax.experimental import pallas as pl
from jax.experimental.pallas import tpu as pltpu
from jax.sharding import PartitionSpec as P

INST = 6
HERE = 3
VARS = 5
FIELDS = HERE * VARS
PLANES = 4
ROWS = 8
NZ = 256
CZ = 128
GROUP = 16
WIN = 2 * GROUP
F32 = jnp.float32
BF16 = jnp.bfloat16


def spectral_matrix():
    rows = np.arange(INST)[:, None]
    cols = np.arange(INST)[None, :]
    diff = rows - cols
    same = diff == 0
    angle = np.where(same, 1.0, np.pi * diff / INST).astype(np.float32)
    signs = np.where(diff % 2 == 0, 1.0, -1.0).astype(np.float32)
    return np.where(same, 0.0, 0.5 * signs * np.cos(angle) / np.sin(angle))


SPECTRAL = spectral_matrix()
OWN = [[float(SPECTRAL[i, j]) for j in range(HERE)] for i in range(HERE)]
OTHER = [[float(SPECTRAL[i, j + HERE]) for j in range(HERE)] for i in range(HERE)]


def tile(field, plane):
    return pl.ds((field * PLANES + plane) * ROWS, ROWS)


def window(plane, field):
    return pl.ds((plane * GROUP + field) * ROWS, ROWS)


def row_of(index):
    return pl.ds(index, WIN, stride=ROWS)


def iota(shape, dim):
    return lax.broadcasted_iota(jnp.int32, shape, dim)


def moved_mask(agg_ref, plane):
    block = agg_ref[pl.ds((2 * plane + 1) * ROWS, ROWS), :]
    own = iota((ROWS, NZ), 0) >> 1
    return (((block >> 7) ^ own) & 1).astype(F32)


def pair_sums(values, ones):
    high = values.astype(BF16)
    low = (values - high.astype(F32)).astype(BF16)
    return jnp.dot(high, ones, preferred_element_type=F32) + jnp.dot(
        low, ones, preferred_element_type=F32
    )


def shift_rows(value, amount):
    return pltpu.roll(value, amount % value.shape[0], 0)


def shift_lanes(value, amount):
    return pltpu.roll(value, amount % value.shape[1], 1)


def even_index(axis):
    return lax.axis_index(axis) % 2 == 0


def choose(flag, value, other):
    return jnp.where(jnp.full(value.shape, flag.astype(jnp.int32)) > 0, value, other)


def edges_kernel(
    state_in, forcing_in, coef_in, agg_in,
    yb, xb, xa, ya, state, forcing, coef, agg, s_win,
    halves, sums, rims, summed, sems,
):
    pairs = ((state_in, state), (coef_in, coef), (agg_in, agg), (forcing_in, forcing))
    copies = [pltpu.make_async_copy(s, d, sems.at[n]) for n, (s, d) in enumerate(pairs)]
    for copy in copies:
        copy.start()
    for copy in copies[:3]:
        copy.wait()
    even_x, even_y = (even_index("sx"), even_index("sy"))
    for field in range(FIELDS):
        high, low = (state[tile(field, PLANES - 1), :], state[tile(field, 0), :])
        xa[pl.ds(field * ROWS, ROWS), :] = choose(even_x, high, low)
        xb[pl.ds(field * ROWS, ROWS), :] = choose(even_x, low, high)
    count = FIELDS * PLANES
    for half in range(2):
        lanes = pl.ds(half * 128, 128)
        halves[half] = state[:, lanes]
        high = halves[half, pl.ds(ROWS - 1, count, stride=ROWS), :]
        low = halves[half, pl.ds(0, count, stride=ROWS), :]
        ya[pl.ds(0, count), lanes] = choose(even_y, high, low)
        yb[pl.ds(0, count), lanes] = choose(even_y, low, high)
        nothing = jnp.zeros((64 - count, 128), F32)
        ya[pl.ds(count, 64 - count), lanes] = nothing
        yb[pl.ds(count, 64 - count), lanes] = nothing
    restrict(state, lambda x: coef[pl.ds(x * ROWS, ROWS), :], agg, s_win, sums, rims, summed)
    for half, (above, below) in enumerate(((5, 2), (6, 1))):
        lanes = pl.ds(half * 128, 128)
        high, low = (s_win[row_of(above), :], s_win[row_of(below), :])
        ya[pl.ds(64, WIN), lanes] = choose(even_y, high, low)
        yb[pl.ds(64, WIN), lanes] = choose(even_y, low, high)
    copies[3].wait()


def split_moved(even, odd, mask, parity, inside):
    moved = odd * mask
    beside = jnp.where(parity, shift_rows(moved, -1), shift_rows(moved, 1))
    return even + (odd - moved) + jnp.where(inside, beside, 0.0), beside


def fill_windows(out, sums, rims, summed, ones):
    summed[pl.ds(0, WIN * ROWS), :] = pair_sums(sums[...], ones)
    first = jnp.concatenate([rims[h, row_of(0), :] for h in range(2)], axis=1)
    last = jnp.concatenate([rims[h, row_of(ROWS - 1), :] for h in range(2)], axis=1)
    rim = pair_sums(jnp.concatenate([first, last], axis=0), ones)
    nothing = jnp.zeros((WIN, CZ), F32)
    out[row_of(0), :] = nothing
    out[row_of(7), :] = nothing
    out[row_of(1), :] = rim[WIN:]
    out[row_of(6), :] = rim[:WIN]
    for b in range(4):
        out[row_of(b + 2), :] = summed[row_of(2 * b), :] + summed[row_of(2 * b + 1), :]


def restrict(fine, last, agg, out, sums, rims, summed):
    row = iota((ROWS, NZ), 0)
    parity = row % 2 == 1
    inside = (row > 0) & (row < ROWS - 1)
    for p in range(2):
        mask = moved_mask(agg, p)
        for field in range(GROUP):
            if field < FIELDS:
                even, odd = (fine[tile(field, 2 * p), :], fine[tile(field, 2 * p + 1), :])
            else:
                even, odd = (last(2 * p), last(2 * p + 1))
            kept, beside = split_moved(even, odd, mask, parity, inside)
            sums[window(p, field), :] = kept
            for half in range(2):
                rims[half, window(p, field), :] = beside[:, half * 128 : (half + 1) * 128]
    fill_windows(out, sums, rims, summed, pair_matrix())


def pair_matrix():
    return (iota((NZ, CZ), 0) >> 1 == iota((NZ, CZ), 1)).astype(BF16)


def inner_kernel(mixing, state, forcing, coef, partial):
    lane = iota((ROWS, NZ), 1)
    row = iota((ROWS, NZ), 0)
    mix = [[mixing[v, w] for w in range(VARS)] for v in range(VARS)]
    for x in range(PLANES):
        c = coef[pl.ds(x * ROWS, ROWS), :]
        for i in range(HERE):
            values = [state[tile(i * VARS + v, x), :] for v in range(VARS)]
            for v in range(VARS):
                field = i * VARS + v
                here = values[v]
                beside = jnp.where(lane == NZ - 1, 0.0, shift_lanes(here, -1))
                beside = beside + jnp.where(lane == 0, 0.0, shift_lanes(here, 1))
                beside = beside + jnp.where(row == ROWS - 1, 0.0, shift_rows(here, -1))
                beside = beside + jnp.where(row == 0, 0.0, shift_rows(here, 1))
                if x > 0:
                    beside = beside + state[tile(field, x - 1), :]
                if x < PLANES - 1:
                    beside = beside + state[tile(field, x + 1), :]
                total = c * (6.0 * here - beside) + jnp.tanh(here)
                for w in range(VARS):
                    total = total + mix[v][w] * values[w]
                for j in range(HERE):
                    if j != i:
                        total = total + OWN[i][j] * state[tile(j * VARS + v, x), :]
                partial[tile(field, x), :] = forcing[tile(field, x), :] - total


def damping(coef_sum, count):
    inverse = jnp.where(count > 0.0, 1.0 / jnp.maximum(count, 1.0), 0.0)
    coef_c = coef_sum * inverse
    return inverse, coef_c, 0.6 / (6.0 * coef_c + 2.0)


def outer_kernel(
    partial, yb, ya, xb, xa, other, coef, agg, s_in,
    mb, ma, residual, r_win, s_win, sums, rims, summed, edge, scaled, halves, coefs,
):
    even_x, even_y = (even_index("sx"), even_index("sy"))
    peer = 1 - lax.axis_index("hb")
    for x in range(PLANES):
        c = coef[pl.ds(x * ROWS, ROWS), :]
        for i in range(HERE):
            for v in range(VARS):
                field = i * VARS + v
                face = pl.ds(field * ROWS, ROWS)
                total = partial[tile(field, x), :]
                for j in range(HERE):
                    total = total - OTHER[i][j] * other[peer, tile(j * VARS + v, x), :]
                if x == 0:
                    total = total + c * choose(even_x, xb[face, :], xa[face, :])
                if x == PLANES - 1:
                    total = total + c * choose(even_x, xa[face, :], xb[face, :])
                for half in range(2):
                    halves[half, tile(field, x), :] = total[:, half * 128 : (half + 1) * 128]
    count = FIELDS * PLANES
    for half in range(2):
        lanes = pl.ds(half * 128, 128)
        coefs[half] = coef[:, lanes]
        at_a, at_b = (ya[pl.ds(0, count), lanes], yb[pl.ds(0, count), lanes])
        for y, halo in ((0, choose(even_y, at_b, at_a)), (ROWS - 1, choose(even_y, at_a, at_b))):
            c4 = coefs[half, pl.ds(y, PLANES, stride=ROWS), :]
            edge[pl.ds(0, PLANES), :] = c4
            edge[pl.ds(PLANES, PLANES), :] = c4
            c8 = edge[...]
            c60 = jnp.concatenate([c8] * (count // 8) + [c8[: count % 8]], axis=0)
            rows = pl.ds(y, count, stride=ROWS)
            halves[half, rows, :] = halves[half, rows, :] + c60 * halo
        residual[:, lanes] = halves[half]
    restrict(residual, lambda x: jnp.ones((ROWS, NZ), F32), agg, r_win, sums, rims, summed)
    s_win[...] = s_in[...]
    for half, (above, below) in enumerate(((6, 1), (5, 2))):
        lanes = pl.ds(half * 128, 128)
        at_a, at_b = (ya[pl.ds(64, WIN), lanes], yb[pl.ds(64, WIN), lanes])
        s_win[row_of(below), :] = s_win[row_of(below), :] + choose(even_y, at_b, at_a)
        s_win[row_of(above), :] = s_win[row_of(above), :] + choose(even_y, at_a, at_b)
    for p in range(2):
        _, _, scale = damping(s_win[window(p, FIELDS), :], r_win[window(p, FIELDS), :])
        for field in range(GROUP):
            scaled[window(p, field), :] = scale * r_win[window(p, field), :]
    pieces = ((scaled, 4, 3), (r_win, 5, 2), (r_win, 6, 1))
    for n, (ref, above, below) in enumerate(pieces):
        high, low = (ref[row_of(above), :], ref[row_of(below), :])
        ma[pl.ds(n * WIN, WIN), :] = choose(even_y, high, low)
        mb[pl.ds(n * WIN, WIN), :] = choose(even_y, low, high)


def store_kernel(values, r_in, out, r_out, sems):
    copy = pltpu.make_async_copy(values, out, sems.at[0])
    copy.start()
    r_out[...] = r_in[...]
    copy.wait()


EDGE_ROWS = 6


def first_kernel(r_in, s_win, mb, ma, xb, xa, delta, r_win):
    even_x, even_y = (even_index("sx"), even_index("sy"))
    r_win[...] = r_in[...]
    pieces = []
    for n in range(3):
        at_a, at_b = (ma[pl.ds(n * WIN, WIN), :], mb[pl.ds(n * WIN, WIN), :])
        pieces.append((choose(even_y, at_b, at_a), choose(even_y, at_a, at_b)))
    for n, below, above in ((1, 1, 6), (2, 2, 5)):
        r_win[row_of(below), :] = r_win[row_of(below), :] + pieces[n][0]
        r_win[row_of(above), :] = r_win[row_of(above), :] + pieces[n][1]
    for p in range(2):
        _, _, scale = damping(s_win[window(p, FIELDS), :], r_win[window(p, FIELDS), :])
        for field in range(GROUP):
            delta[window(p, field), :] = scale * r_win[window(p, field), :]
    delta[row_of(0), :] = pieces[0][0]
    delta[row_of(7), :] = pieces[0][1]
    for r in range(EDGE_ROWS):
        low = delta[pl.ds(r + 1, GROUP, stride=ROWS), :]
        high = delta[pl.ds(GROUP * ROWS + r + 1, GROUP, stride=ROWS), :]
        xa[pl.ds(r * GROUP, GROUP), :] = choose(even_x, high, low)
        xb[pl.ds(r * GROUP, GROUP), :] = choose(even_x, low, high)


def second_kernel(mixing, r_win, s_win, delta, partial):
    lane = iota((ROWS, CZ), 1)
    mix = [[mixing[v, w] for w in range(VARS)] for v in range(VARS)]
    for p in range(2):
        inverse, coef_c, scale = damping(s_win[window(p, FIELDS), :], r_win[window(p, FIELDS), :])
        for i in range(HERE):
            values = [delta[window(p, i * VARS + v), :] for v in range(VARS)]
            for v in range(VARS):
                field = i * VARS + v
                here = values[v]
                beside = jnp.where(lane == CZ - 1, 0.0, shift_lanes(here, -1))
                beside = beside + jnp.where(lane == 0, 0.0, shift_lanes(here, 1))
                beside = beside + shift_rows(here, -1) + shift_rows(here, 1)
                beside = beside + delta[window(1 - p, field), :]
                total = coef_c * (6.0 * here - beside)
                start = s_win[window(p, field), :] * inverse
                total = total + (jnp.tanh(start + here) - jnp.tanh(start))
                for w in range(VARS):
                    total = total + mix[v][w] * values[w]
                for j in range(HERE):
                    if j != i:
                        total = total + OWN[i][j] * delta[window(p, j * VARS + v), :]
                partial[window(p, field), :] = here + scale * (r_win[window(p, field), :] - total)
        partial[window(p, FIELDS), :] = coef_c


def final_kernel(
    partial, xb, xa, other, state, agg, corrected, change, fine, own, beside, halos, result, sems
):
    even_x = even_index("sx")
    peer = 1 - lax.axis_index("hb")
    for r in range(EDGE_ROWS):
        at_a, at_b = (xa[pl.ds(r * GROUP, GROUP), :], xb[pl.ds(r * GROUP, GROUP), :])
        rows = pl.ds(r + 1, GROUP, stride=ROWS)
        halos[0, rows, :] = choose(even_x, at_b, at_a)
        halos[1, rows, :] = choose(even_x, at_a, at_b)
    for p in range(2):
        for r in (0, ROWS - 1):
            halos[p, pl.ds(r, GROUP, stride=ROWS), :] = jnp.zeros((GROUP, CZ), F32)
    for p in range(2):
        coef_c = partial[window(p, FIELDS), :]
        scale = 0.6 / (6.0 * coef_c + 2.0)
        for i in range(HERE):
            for v in range(VARS):
                field = i * VARS + v
                total = coef_c * halos[p, pl.ds(field * ROWS, ROWS), :]
                for j in range(HERE):
                    total = total - OTHER[i][j] * other[peer, window(p, j * VARS + v), :]
                change[window(p, field), :] = partial[window(p, field), :] + scale * total
        change[window(p, FIELDS), :] = jnp.zeros((ROWS, CZ), F32)
    twice = (iota((CZ, NZ), 1) >> 1 == iota((CZ, NZ), 0)).astype(BF16)
    for half in range(2):
        fine[half] = pair_sums(change[...], twice[:, half * 128 : (half + 1) * 128])
    for half in range(2):
        rows = [fine[half, row_of(b + 1), :] for b in range(6)]
        for b in range(4):
            own[half, row_of(2 * b), :] = rows[b + 1]
            own[half, row_of(2 * b + 1), :] = rows[b + 1]
            beside[half, row_of(2 * b), :] = rows[b]
            beside[half, row_of(2 * b + 1), :] = rows[b + 2]
    masks = [moved_mask(agg, p) > 0.0 for p in range(2)]
    copies = []
    for i in range(HERE):
        for field in range(i * VARS, (i + 1) * VARS):
            for p in range(2):
                for half in range(2):
                    lanes = pl.ds(half * 128, 128)
                    moved = masks[p][:, half * 128 : (half + 1) * 128]
                    kept = own[half, window(p, field), :]
                    went = beside[half, window(p, field), :]
                    even, odd = (tile(field, 2 * p), tile(field, 2 * p + 1))
                    result[even, lanes] = state[even, lanes] + kept
                    result[odd, lanes] = state[odd, lanes] + jnp.where(moved, went, kept)
        rows = pl.ds(i * VARS * PLANES * ROWS, VARS * PLANES * ROWS)
        copies.append(pltpu.make_async_copy(result.at[rows, :], corrected.at[rows, :], sems.at[i]))
        copies[-1].start()
    for copy in copies:
        copy.wait()


VMEM = pl.BlockSpec(memory_space=pltpu.VMEM)
SMEM = pl.BlockSpec(memory_space=pltpu.SMEM)
HBM = pl.BlockSpec(memory_space=pltpu.HBM)


def call(kernel, outs, scratch, *args, spaces=(), out_space=VMEM, sems=0):
    spaces = list(spaces) + [VMEM] * (len(args) - len(spaces))
    args = [
        pltpu.with_memory_space_constraint(a, pltpu.HBM) if s is HBM else a
        for a, s in zip(args, spaces)
    ]
    outs = [o if hasattr(o, "dtype") else jax.ShapeDtypeStruct(o, F32) for o in outs]
    return pl.pallas_call(
        kernel,
        out_shape=outs,
        in_specs=spaces,
        out_specs=out_space if isinstance(out_space, list) else [out_space] * len(outs),
        scratch_shapes=[pltpu.VMEM(s, F32) for s in scratch]
        + ([pltpu.SemaphoreType.DMA((sems,))] if sems else []),
        compiler_params=pltpu.CompilerParams(vmem_limit_bytes=40 * 1024 * 1024),
        name=kernel.__name__,
    )(*args)


def swap_pairs(axis, first):
    size = lax.axis_size(axis)
    up = [(i, i + 1) for i in range(first, size - 1, 2)]
    return up + [(j, i) for i, j in up]


def shards(state, forcing, coef, mixing, agglomerate):
    shape = state.shape
    fine = (FIELDS * PLANES * ROWS, NZ)
    wins = (WIN * ROWS, CZ)
    state = state.reshape(fine)
    forcing = forcing.reshape(fine)
    coef = coef.reshape(PLANES * ROWS, NZ)
    agg = agglomerate.reshape(PLANES * ROWS, NZ)

    def swap(value, axis, first=0):
        return lax.ppermute(value, axis, swap_pairs(axis, first))

    halves = (2, FIELDS * PLANES * ROWS, 128)
    sums = (WIN * ROWS, NZ)
    rims = (2, WIN * ROWS, 128)
    x_face = (FIELDS * ROWS, NZ)
    y_face = (120, NZ)
    yb, xb, xa, ya, state, forcing, coef, agg, s_win = call(
        edges_kernel,
        [y_face, x_face, x_face, y_face, fine, fine, coef.shape, agg, wins],
        [halves, sums, rims, wins],
        state, forcing, coef, agg,
        spaces=[HBM] * 4,
        sems=4,
    )
    yb = swap(yb, "sy", 1)
    xb = swap(xb, "sx", 1)
    xa = swap(xa, "sx")
    ya = swap(ya, "sy")
    other = lax.all_gather(state, "hb")
    (partial,) = call(inner_kernel, [fine], [], mixing, state, forcing, coef, spaces=[SMEM])
    msg = (3 * WIN, CZ)
    mb, ma, residual, r_win, s_win = call(
        outer_kernel,
        [msg, msg, fine, wins, wins],
        [sums, rims, wins, (8, 128), wins, halves, (2, PLANES * ROWS, 128)],
        partial, yb, ya, xb, xa, other, coef, agg, s_win,
    )
    mb = swap(mb, "sy", 1)
    ma = swap(ma, "sy")
    residual, r_win = call(
        store_kernel, [fine, wins], [], residual, r_win, out_space=[HBM, VMEM], sems=1
    )
    face = (EDGE_ROWS * GROUP, CZ)
    db, da, delta, r_win = call(
        first_kernel, [face, face, wins, wins], [], r_win, s_win, mb, ma
    )
    db = swap(db, "sx", 1)
    da = swap(da, "sx")
    other_delta = lax.all_gather(delta, "hb")
    (step,) = call(second_kernel, [wins], [], mixing, r_win, s_win, delta, spaces=[SMEM])
    (corrected,) = call(
        final_kernel,
        [fine],
        [wins, (2,) + wins, (2,) + wins, (2,) + wins, (2, GROUP * ROWS, CZ), fine],
        step, db, da, other_delta, state, agg,
        out_space=HBM,
        sems=HERE,
    )
    return corrected.reshape(shape), residual.reshape(shape)


def solution(mesh):
    whole = P("hb", None, "sx", "sy", None)
    return jax.shard_map(
        shards,
        mesh=mesh,
        in_specs=(whole, whole, P("sx", "sy", None), P(), P("sx", "sy", None)),
        out_specs=(whole, whole),
        check_vma=False,
    )
```

```python
import functools

import jax
import jax.numpy as jnp
import numpy as np
from jax import lax
from jax.experimental import pallas as pl
from jax.experimental.pallas import tpu as pltpu
from jax.sharding import PartitionSpec as P

INST = 6
HERE = 3
VARS = 5
FIELDS = HERE * VARS
PLANES = 4
ROWS = 8
NZ = 256
CZ = 128
GROUP = 16
WIN = 2 * GROUP
F32 = jnp.float32
BF16 = jnp.bfloat16


def spectral_matrix():
    rows = np.arange(INST)[:, None]
    cols = np.arange(INST)[None, :]
    diff = rows - cols
    same = diff == 0
    angle = np.where(same, 1.0, np.pi * diff / INST).astype(np.float32)
    signs = np.where(diff % 2 == 0, 1.0, -1.0).astype(np.float32)
    return np.where(same, 0.0, 0.5 * signs * np.cos(angle) / np.sin(angle))


SPECTRAL = spectral_matrix()
OWN = [[float(SPECTRAL[i, j]) for j in range(HERE)] for i in range(HERE)]
OTHER = [[float(SPECTRAL[i, j + HERE]) for j in range(HERE)] for i in range(HERE)]


def tile(field, plane):
    return pl.ds((field * PLANES + plane) * ROWS, ROWS)


def window(plane, field):
    return pl.ds((plane * GROUP + field) * ROWS, ROWS)


def row_of(index):
    return pl.ds(index, WIN, stride=ROWS)


def iota(shape, dim):
    return lax.broadcasted_iota(jnp.int32, shape, dim)


def spread(mixing, lanes):
    return [
        [jnp.broadcast_to(mixing[pl.ds(v, 1), pl.ds(w, 1)], (ROWS, lanes)) for w in range(VARS)]
        for v in range(VARS)
    ]


def moved_mask(agg_ref, plane):
    block = agg_ref[pl.ds((2 * plane + 1) * ROWS, ROWS), :]
    own = iota((ROWS, NZ), 0) >> 1
    return (((block >> 7) ^ own) & 1).astype(F32)


def pair_sums(values, ones):
    high = values.astype(BF16)
    low = (values - high.astype(F32)).astype(BF16)
    return jnp.dot(high, ones, preferred_element_type=F32) + jnp.dot(
        low, ones, preferred_element_type=F32
    )


def shift_rows(value, amount):
    return pltpu.roll(value, amount % value.shape[0], 0)


def shift_lanes(value, amount):
    return pltpu.roll(value, amount % value.shape[1], 1)


def even_index(axis):
    return lax.axis_index(axis) % 2 == 0


def choose(flag, value, other):
    return jnp.where(jnp.full(value.shape, flag.astype(jnp.int32)) > 0, value, other)


def edges_kernel(
    state_in, forcing_in, coef_in, agg_in,
    yb, xb, xa, ya, state, forcing, coef, agg, s_win,
    halves, sums, rims, summed, sems,
):
    pairs = ((state_in, state), (coef_in, coef), (agg_in, agg), (forcing_in, forcing))
    copies = [pltpu.make_async_copy(s, d, sems.at[n]) for n, (s, d) in enumerate(pairs)]
    for copy in copies:
        copy.start()
    for copy in copies[:3]:
        copy.wait()
    even_x, even_y = (even_index("sx"), even_index("sy"))
    for field in range(FIELDS):
        high, low = (state[tile(field, PLANES - 1), :], state[tile(field, 0), :])
        xa[pl.ds(field * ROWS, ROWS), :] = choose(even_x, high, low)
        xb[pl.ds(field * ROWS, ROWS), :] = choose(even_x, low, high)
    count = FIELDS * PLANES
    for half in range(2):
        lanes = pl.ds(half * 128, 128)
        halves[half] = state[:, lanes]
        high = halves[half, pl.ds(ROWS - 1, count, stride=ROWS), :]
        low = halves[half, pl.ds(0, count, stride=ROWS), :]
        ya[pl.ds(0, count), lanes] = choose(even_y, high, low)
        yb[pl.ds(0, count), lanes] = choose(even_y, low, high)
        nothing = jnp.zeros((64 - count, 128), F32)
        ya[pl.ds(count, 64 - count), lanes] = nothing
        yb[pl.ds(count, 64 - count), lanes] = nothing
    restrict(state, lambda x: coef[pl.ds(x * ROWS, ROWS), :], agg, s_win, sums, rims, summed)
    for half, (above, below) in enumerate(((5, 2), (6, 1))):
        lanes = pl.ds(half * 128, 128)
        high, low = (s_win[row_of(above), :], s_win[row_of(below), :])
        ya[pl.ds(64, WIN), lanes] = choose(even_y, high, low)
        yb[pl.ds(64, WIN), lanes] = choose(even_y, low, high)
    copies[3].wait()


def split_moved(even, odd, mask, parity, inside):
    moved = odd * mask
    beside = jnp.where(parity, shift_rows(moved, -1), shift_rows(moved, 1))
    return even + (odd - moved) + jnp.where(inside, beside, 0.0), beside


def fill_windows(out, sums, rims, summed, ones):
    summed[pl.ds(0, WIN * ROWS), :] = pair_sums(sums[...], ones)
    first = jnp.concatenate([rims[h, row_of(0), :] for h in range(2)], axis=1)
    last = jnp.concatenate([rims[h, row_of(ROWS - 1), :] for h in range(2)], axis=1)
    rim = pair_sums(jnp.concatenate([first, last], axis=0), ones)
    nothing = jnp.zeros((WIN, CZ), F32)
    out[row_of(0), :] = nothing
    out[row_of(7), :] = nothing
    out[row_of(1), :] = rim[WIN:]
    out[row_of(6), :] = rim[:WIN]
    for b in range(4):
        out[row_of(b + 2), :] = summed[row_of(2 * b), :] + summed[row_of(2 * b + 1), :]


def restrict(fine, last, agg, out, sums, rims, summed):
    row = iota((ROWS, NZ), 0)
    parity = row % 2 == 1
    inside = (row > 0) & (row < ROWS - 1)
    for p in range(2):
        mask = moved_mask(agg, p)
        for field in range(GROUP):
            if field < FIELDS:
                even, odd = (fine[tile(field, 2 * p), :], fine[tile(field, 2 * p + 1), :])
            else:
                even, odd = (last(2 * p), last(2 * p + 1))
            kept, beside = split_moved(even, odd, mask, parity, inside)
            sums[window(p, field), :] = kept
            for half in range(2):
                rims[half, window(p, field), :] = beside[:, half * 128 : (half + 1) * 128]
    fill_windows(out, sums, rims, summed, pair_matrix())


def pair_matrix():
    return (iota((NZ, CZ), 0) >> 1 == iota((NZ, CZ), 1)).astype(BF16)


def inner_kernel(mixing, state, forcing, coef, partial):
    lane = iota((ROWS, NZ), 1)
    row = iota((ROWS, NZ), 0)
    mix = spread(mixing, NZ)
    for x in range(PLANES):
        c = coef[pl.ds(x * ROWS, ROWS), :]
        for i in range(HERE):
            values = [state[tile(i * VARS + v, x), :] for v in range(VARS)]
            for v in range(VARS):
                field = i * VARS + v
                here = values[v]
                beside = jnp.where(lane == NZ - 1, 0.0, shift_lanes(here, -1))
                beside = beside + jnp.where(lane == 0, 0.0, shift_lanes(here, 1))
                beside = beside + jnp.where(row == ROWS - 1, 0.0, shift_rows(here, -1))
                beside = beside + jnp.where(row == 0, 0.0, shift_rows(here, 1))
                if x > 0:
                    beside = beside + state[tile(field, x - 1), :]
                if x < PLANES - 1:
                    beside = beside + state[tile(field, x + 1), :]
                total = c * (6.0 * here - beside) + jnp.tanh(here)
                for w in range(VARS):
                    total = total + mix[v][w] * values[w]
                for j in range(HERE):
                    if j != i:
                        total = total + OWN[i][j] * state[tile(j * VARS + v, x), :]
                partial[tile(field, x), :] = forcing[tile(field, x), :] - total


def damping(coef_sum, count):
    inverse = jnp.where(count > 0.0, 1.0 / jnp.maximum(count, 1.0), 0.0)
    coef_c = coef_sum * inverse
    return inverse, coef_c, 0.6 / (6.0 * coef_c + 2.0)


def outer_kernel(
    partial, yb, ya, xb, xa, other, coef, agg, s_in,
    mb, ma, residual, r_win, s_win, sums, rims, summed, edge, scaled, halves, coefs,
):
    even_x, even_y = (even_index("sx"), even_index("sy"))
    peer = 1 - lax.axis_index("hb")
    for x in range(PLANES):
        c = coef[pl.ds(x * ROWS, ROWS), :]
        for i in range(HERE):
            for v in range(VARS):
                field = i * VARS + v
                face = pl.ds(field * ROWS, ROWS)
                total = partial[tile(field, x), :]
                for j in range(HERE):
                    total = total - OTHER[i][j] * other[peer, tile(j * VARS + v, x), :]
                if x == 0:
                    total = total + c * choose(even_x, xb[face, :], xa[face, :])
                if x == PLANES - 1:
                    total = total + c * choose(even_x, xa[face, :], xb[face, :])
                for half in range(2):
                    halves[half, tile(field, x), :] = total[:, half * 128 : (half + 1) * 128]
    count = FIELDS * PLANES
    for half in range(2):
        lanes = pl.ds(half * 128, 128)
        coefs[half] = coef[:, lanes]
        at_a, at_b = (ya[pl.ds(0, count), lanes], yb[pl.ds(0, count), lanes])
        for y, halo in ((0, choose(even_y, at_b, at_a)), (ROWS - 1, choose(even_y, at_a, at_b))):
            c4 = coefs[half, pl.ds(y, PLANES, stride=ROWS), :]
            edge[pl.ds(0, PLANES), :] = c4
            edge[pl.ds(PLANES, PLANES), :] = c4
            c8 = edge[...]
            c60 = jnp.concatenate([c8] * (count // 8) + [c8[: count % 8]], axis=0)
            rows = pl.ds(y, count, stride=ROWS)
            halves[half, rows, :] = halves[half, rows, :] + c60 * halo
        residual[:, lanes] = halves[half]
    restrict(residual, lambda x: jnp.ones((ROWS, NZ), F32), agg, r_win, sums, rims, summed)
    s_win[...] = s_in[...]
    for half, (above, below) in enumerate(((6, 1), (5, 2))):
        lanes = pl.ds(half * 128, 128)
        at_a, at_b = (ya[pl.ds(64, WIN), lanes], yb[pl.ds(64, WIN), lanes])
        s_win[row_of(below), :] = s_win[row_of(below), :] + choose(even_y, at_b, at_a)
        s_win[row_of(above), :] = s_win[row_of(above), :] + choose(even_y, at_a, at_b)
    for p in range(2):
        _, _, scale = damping(s_win[window(p, FIELDS), :], r_win[window(p, FIELDS), :])
        for field in range(GROUP):
            scaled[window(p, field), :] = scale * r_win[window(p, field), :]
    pieces = ((scaled, 4, 3), (r_win, 5, 2), (r_win, 6, 1))
    for n, (ref, above, below) in enumerate(pieces):
        high, low = (ref[row_of(above), :], ref[row_of(below), :])
        ma[pl.ds(n * WIN, WIN), :] = choose(even_y, high, low)
        mb[pl.ds(n * WIN, WIN), :] = choose(even_y, low, high)


def store_kernel(values, r_in, out, r_out, sems):
    copy = pltpu.make_async_copy(values, out, sems.at[0])
    copy.start()
    r_out[...] = r_in[...]
    copy.wait()


EDGE_ROWS = 6


def first_kernel(r_in, s_win, mb, ma, xb, xa, delta, r_win):
    even_x, even_y = (even_index("sx"), even_index("sy"))
    r_win[...] = r_in[...]
    pieces = []
    for n in range(3):
        at_a, at_b = (ma[pl.ds(n * WIN, WIN), :], mb[pl.ds(n * WIN, WIN), :])
        pieces.append((choose(even_y, at_b, at_a), choose(even_y, at_a, at_b)))
    for n, below, above in ((1, 1, 6), (2, 2, 5)):
        r_win[row_of(below), :] = r_win[row_of(below), :] + pieces[n][0]
        r_win[row_of(above), :] = r_win[row_of(above), :] + pieces[n][1]
    for p in range(2):
        _, _, scale = damping(s_win[window(p, FIELDS), :], r_win[window(p, FIELDS), :])
        for field in range(GROUP):
            delta[window(p, field), :] = scale * r_win[window(p, field), :]
    delta[row_of(0), :] = pieces[0][0]
    delta[row_of(7), :] = pieces[0][1]
    for r in range(EDGE_ROWS):
        low = delta[pl.ds(r + 1, GROUP, stride=ROWS), :]
        high = delta[pl.ds(GROUP * ROWS + r + 1, GROUP, stride=ROWS), :]
        xa[pl.ds(r * GROUP, GROUP), :] = choose(even_x, high, low)
        xb[pl.ds(r * GROUP, GROUP), :] = choose(even_x, low, high)


def second_kernel(mixing, r_win, s_win, delta, partial):
    lane = iota((ROWS, CZ), 1)
    mix = spread(mixing, CZ)
    for p in range(2):
        inverse, coef_c, scale = damping(s_win[window(p, FIELDS), :], r_win[window(p, FIELDS), :])
        for i in range(HERE):
            values = [delta[window(p, i * VARS + v), :] for v in range(VARS)]
            for v in range(VARS):
                field = i * VARS + v
                here = values[v]
                beside = jnp.where(lane == CZ - 1, 0.0, shift_lanes(here, -1))
                beside = beside + jnp.where(lane == 0, 0.0, shift_lanes(here, 1))
                beside = beside + shift_rows(here, -1) + shift_rows(here, 1)
                beside = beside + delta[window(1 - p, field), :]
                total = coef_c * (6.0 * here - beside)
                start = s_win[window(p, field), :] * inverse
                total = total + (jnp.tanh(start + here) - jnp.tanh(start))
                for w in range(VARS):
                    total = total + mix[v][w] * values[w]
                for j in range(HERE):
                    if j != i:
                        total = total + OWN[i][j] * delta[window(p, j * VARS + v), :]
                partial[window(p, field), :] = here + scale * (r_win[window(p, field), :] - total)
        partial[window(p, FIELDS), :] = coef_c


def final_kernel(
    partial, xb, xa, other, state, agg, corrected, change, fine, own, beside, halos, result, sems
):
    even_x = even_index("sx")
    peer = 1 - lax.axis_index("hb")
    for r in range(EDGE_ROWS):
        at_a, at_b = (xa[pl.ds(r * GROUP, GROUP), :], xb[pl.ds(r * GROUP, GROUP), :])
        rows = pl.ds(r + 1, GROUP, stride=ROWS)
        halos[0, rows, :] = choose(even_x, at_b, at_a)
        halos[1, rows, :] = choose(even_x, at_a, at_b)
    for p in range(2):
        for r in (0, ROWS - 1):
            halos[p, pl.ds(r, GROUP, stride=ROWS), :] = jnp.zeros((GROUP, CZ), F32)
    for p in range(2):
        coef_c = partial[window(p, FIELDS), :]
        scale = 0.6 / (6.0 * coef_c + 2.0)
        for i in range(HERE):
            for v in range(VARS):
                field = i * VARS + v
                total = coef_c * halos[p, pl.ds(field * ROWS, ROWS), :]
                for j in range(HERE):
                    total = total - OTHER[i][j] * other[peer, window(p, j * VARS + v), :]
                change[window(p, field), :] = partial[window(p, field), :] + scale * total
        change[window(p, FIELDS), :] = jnp.zeros((ROWS, CZ), F32)
    twice = (iota((CZ, NZ), 1) >> 1 == iota((CZ, NZ), 0)).astype(BF16)
    for half in range(2):
        fine[half] = pair_sums(change[...], twice[:, half * 128 : (half + 1) * 128])
    for half in range(2):
        rows = [fine[half, row_of(b + 1), :] for b in range(6)]
        for b in range(4):
            own[half, row_of(2 * b), :] = rows[b + 1]
            own[half, row_of(2 * b + 1), :] = rows[b + 1]
            beside[half, row_of(2 * b), :] = rows[b]
            beside[half, row_of(2 * b + 1), :] = rows[b + 2]
    masks = [moved_mask(agg, p) > 0.0 for p in range(2)]
    copies = []
    for i in range(HERE):
        for field in range(i * VARS, (i + 1) * VARS):
            for p in range(2):
                for half in range(2):
                    lanes = pl.ds(half * 128, 128)
                    moved = masks[p][:, half * 128 : (half + 1) * 128]
                    kept = own[half, window(p, field), :]
                    went = beside[half, window(p, field), :]
                    even, odd = (tile(field, 2 * p), tile(field, 2 * p + 1))
                    result[even, lanes] = state[even, lanes] + kept
                    result[odd, lanes] = state[odd, lanes] + jnp.where(moved, went, kept)
        rows = pl.ds(i * VARS * PLANES * ROWS, VARS * PLANES * ROWS)
        copies.append(pltpu.make_async_copy(result.at[rows, :], corrected.at[rows, :], sems.at[i]))
        copies[-1].start()
    for copy in copies:
        copy.wait()


VMEM = pl.BlockSpec(memory_space=pltpu.VMEM)
HBM = pl.BlockSpec(memory_space=pltpu.HBM)


def call(kernel, outs, scratch, *args, spaces=(), out_space=VMEM, sems=0):
    spaces = list(spaces) + [VMEM] * (len(args) - len(spaces))
    args = [
        pltpu.with_memory_space_constraint(a, pltpu.HBM) if s is HBM else a
        for a, s in zip(args, spaces)
    ]
    outs = [o if hasattr(o, "dtype") else jax.ShapeDtypeStruct(o, F32) for o in outs]
    return pl.pallas_call(
        kernel,
        out_shape=outs,
        in_specs=spaces,
        out_specs=out_space if isinstance(out_space, list) else [out_space] * len(outs),
        scratch_shapes=[pltpu.VMEM(s, F32) for s in scratch]
        + ([pltpu.SemaphoreType.DMA((sems,))] if sems else []),
        compiler_params=pltpu.CompilerParams(vmem_limit_bytes=40 * 1024 * 1024),
        name=kernel.__name__,
    )(*args)


def swap_pairs(axis, first):
    size = lax.axis_size(axis)
    up = [(i, i + 1) for i in range(first, size - 1, 2)]
    return up + [(j, i) for i, j in up]


def shards(state, forcing, coef, mixing, agglomerate):
    shape = state.shape
    fine = (FIELDS * PLANES * ROWS, NZ)
    wins = (WIN * ROWS, CZ)
    state = state.reshape(fine)
    forcing = forcing.reshape(fine)
    coef = coef.reshape(PLANES * ROWS, NZ)
    agg = agglomerate.reshape(PLANES * ROWS, NZ)

    def swap(value, axis, first=0):
        return lax.ppermute(value, axis, swap_pairs(axis, first))

    halves = (2, FIELDS * PLANES * ROWS, 128)
    sums = (WIN * ROWS, NZ)
    rims = (2, WIN * ROWS, 128)
    x_face = (FIELDS * ROWS, NZ)
    y_face = (64 + WIN, NZ)
    yb, xb, xa, ya, state, forcing, coef, agg, s_win = call(
        edges_kernel,
        [y_face, x_face, x_face, y_face, fine, fine, coef.shape, agg, wins],
        [halves, sums, rims, wins],
        state, forcing, coef, agg,
        spaces=[HBM] * 4,
        sems=4,
    )
    yb = swap(yb, "sy", 1)
    xb = swap(xb, "sx", 1)
    xa = swap(xa, "sx")
    ya = swap(ya, "sy")
    other = lax.all_gather(state, "hb")
    (partial,) = call(inner_kernel, [fine], [], mixing, state, forcing, coef)
    msg = (3 * WIN, CZ)
    mb, ma, residual, r_win, s_win = call(
        outer_kernel,
        [msg, msg, fine, wins, wins],
        [sums, rims, wins, (8, 128), wins, halves, (2, PLANES * ROWS, 128)],
        partial, yb, ya, xb, xa, other, coef, agg, s_win,
    )
    mb = swap(mb, "sy", 1)
    ma = swap(ma, "sy")
    residual, r_win = call(
        store_kernel, [fine, wins], [], residual, r_win, out_space=[HBM, VMEM], sems=1
    )
    face = (EDGE_ROWS * GROUP, CZ)
    db, da, delta, r_win = call(
        first_kernel, [face, face, wins, wins], [], r_win, s_win, mb, ma
    )
    db = swap(db, "sx", 1)
    da = swap(da, "sx")
    other_delta = lax.all_gather(delta, "hb")
    (step,) = call(second_kernel, [wins], [], mixing, r_win, s_win, delta)
    (corrected,) = call(
        final_kernel,
        [fine],
        [wins, (2,) + wins, (2,) + wins, (2,) + wins, (2, GROUP * ROWS, CZ), fine],
        step, db, da, other_delta, state, agg,
        out_space=HBM,
        sems=HERE,
    )
    return corrected.reshape(shape), residual.reshape(shape)


def solution(mesh):
    whole = P("hb", None, "sx", "sy", None)
    return jax.shard_map(
        shards,
        mesh=mesh,
        in_specs=(whole, whole, P("sx", "sy", None), P(), P("sx", "sy", None)),
        out_specs=(whole, whole),
        check_vma=False,
    )
```

```python
import functools

import jax
import jax.numpy as jnp
import numpy as np
from jax import lax
from jax.experimental import pallas as pl
from jax.experimental.pallas import tpu as pltpu
from jax.sharding import PartitionSpec as P

INST = 6
HERE = 3
VARS = 5
FIELDS = HERE * VARS
PLANES = 4
ROWS = 8
NZ = 256
CZ = 128
GROUP = 16
WIN = 2 * GROUP
F32 = jnp.float32
BF16 = jnp.bfloat16


def spectral_matrix():
    rows = np.arange(INST)[:, None]
    cols = np.arange(INST)[None, :]
    diff = rows - cols
    same = diff == 0
    angle = np.where(same, 1.0, np.pi * diff / INST).astype(np.float32)
    signs = np.where(diff % 2 == 0, 1.0, -1.0).astype(np.float32)
    return np.where(same, 0.0, 0.5 * signs * np.cos(angle) / np.sin(angle))


SPECTRAL = spectral_matrix()
OWN = [[float(SPECTRAL[i, j]) for j in range(HERE)] for i in range(HERE)]
OTHER = [[float(SPECTRAL[i, j + HERE]) for j in range(HERE)] for i in range(HERE)]


def tile(field, plane):
    return pl.ds((field * PLANES + plane) * ROWS, ROWS)


def window(plane, field):
    return pl.ds((plane * GROUP + field) * ROWS, ROWS)


def row_of(index):
    return pl.ds(index, WIN, stride=ROWS)


def iota(shape, dim):
    return lax.broadcasted_iota(jnp.int32, shape, dim)


def spread(mixing, lanes):
    return [
        [jnp.broadcast_to(mixing[pl.ds(v, 1), pl.ds(w, 1)], (ROWS, lanes)) for w in range(VARS)]
        for v in range(VARS)
    ]


def moved_mask(agg_ref, plane):
    block = agg_ref[pl.ds((2 * plane + 1) * ROWS, ROWS), :]
    own = iota((ROWS, NZ), 0) >> 1
    return (((block >> 7) ^ own) & 1).astype(F32)


def pair_sums(values, ones):
    high = values.astype(BF16)
    low = (values - high.astype(F32)).astype(BF16)
    return jnp.dot(high, ones, preferred_element_type=F32) + jnp.dot(
        low, ones, preferred_element_type=F32
    )


def shift_rows(value, amount):
    return pltpu.roll(value, amount % value.shape[0], 0)


def shift_lanes(value, amount):
    return pltpu.roll(value, amount % value.shape[1], 1)


def even_index(axis):
    return lax.axis_index(axis) % 2 == 0


def choose(flag, value, other):
    return jnp.where(jnp.full(value.shape, flag.astype(jnp.int32)) > 0, value, other)


def edges_kernel(
    state_in, forcing_in, coef_in, agg_in,
    yb, xb, xa, ya, state, forcing, coef, agg, s_win,
    halves, sums, rims, summed, sems,
):
    pairs = ((state_in, state), (coef_in, coef), (agg_in, agg), (forcing_in, forcing))
    copies = [pltpu.make_async_copy(s, d, sems.at[n]) for n, (s, d) in enumerate(pairs)]
    for copy in copies:
        copy.start()
    for copy in copies[:3]:
        copy.wait()
    even_x, even_y = (even_index("sx"), even_index("sy"))
    for field in range(FIELDS):
        high, low = (state[tile(field, PLANES - 1), :], state[tile(field, 0), :])
        xa[pl.ds(field * ROWS, ROWS), :] = choose(even_x, high, low)
        xb[pl.ds(field * ROWS, ROWS), :] = choose(even_x, low, high)
    count = FIELDS * PLANES
    for half in range(2):
        lanes = pl.ds(half * 128, 128)
        halves[half] = state[:, lanes]
        high = halves[half, pl.ds(ROWS - 1, count, stride=ROWS), :]
        low = halves[half, pl.ds(0, count, stride=ROWS), :]
        ya[pl.ds(0, count), lanes] = choose(even_y, high, low)
        yb[pl.ds(0, count), lanes] = choose(even_y, low, high)
        nothing = jnp.zeros((64 - count, 128), F32)
        ya[pl.ds(count, 64 - count), lanes] = nothing
        yb[pl.ds(count, 64 - count), lanes] = nothing
    restrict(state, lambda x: coef[pl.ds(x * ROWS, ROWS), :], agg, s_win, sums, rims, summed)
    for half, (above, below) in enumerate(((5, 2), (6, 1))):
        lanes = pl.ds(half * 128, 128)
        high, low = (s_win[row_of(above), :], s_win[row_of(below), :])
        ya[pl.ds(64, WIN), lanes] = choose(even_y, high, low)
        yb[pl.ds(64, WIN), lanes] = choose(even_y, low, high)
    copies[3].wait()


def split_moved(even, odd, mask, parity, inside):
    moved = odd * mask
    beside = jnp.where(parity, shift_rows(moved, -1), shift_rows(moved, 1))
    return even + (odd - moved) + jnp.where(inside, beside, 0.0), beside


def fill_windows(out, sums, rims, summed, ones):
    summed[pl.ds(0, WIN * ROWS), :] = pair_sums(sums[...], ones)
    first = jnp.concatenate([rims[h, row_of(0), :] for h in range(2)], axis=1)
    last = jnp.concatenate([rims[h, row_of(ROWS - 1), :] for h in range(2)], axis=1)
    rim = pair_sums(jnp.concatenate([first, last], axis=0), ones)
    nothing = jnp.zeros((WIN, CZ), F32)
    out[row_of(0), :] = nothing
    out[row_of(7), :] = nothing
    out[row_of(1), :] = rim[WIN:]
    out[row_of(6), :] = rim[:WIN]
    for b in range(4):
        out[row_of(b + 2), :] = summed[row_of(2 * b), :] + summed[row_of(2 * b + 1), :]


def restrict(fine, last, agg, out, sums, rims, summed):
    row = iota((ROWS, NZ), 0)
    parity = row % 2 == 1
    inside = (row > 0) & (row < ROWS - 1)
    for p in range(2):
        mask = moved_mask(agg, p)
        for field in range(GROUP):
            if field < FIELDS:
                even, odd = (fine[tile(field, 2 * p), :], fine[tile(field, 2 * p + 1), :])
            else:
                even, odd = (last(2 * p), last(2 * p + 1))
            kept, beside = split_moved(even, odd, mask, parity, inside)
            sums[window(p, field), :] = kept
            for half in range(2):
                rims[half, window(p, field), :] = beside[:, half * 128 : (half + 1) * 128]
    fill_windows(out, sums, rims, summed, pair_matrix())


def pair_matrix():
    return (iota((NZ, CZ), 0) >> 1 == iota((NZ, CZ), 1)).astype(BF16)


def inner_kernel(mixing, state, forcing, coef, partial):
    lane = iota((ROWS, NZ), 1)
    row = iota((ROWS, NZ), 0)
    mix = spread(mixing, NZ)
    for x in range(PLANES):
        c = coef[pl.ds(x * ROWS, ROWS), :]
        for i in range(HERE):
            values = [state[tile(i * VARS + v, x), :] for v in range(VARS)]
            for v in range(VARS):
                field = i * VARS + v
                here = values[v]
                beside = jnp.where(lane == NZ - 1, 0.0, shift_lanes(here, -1))
                beside = beside + jnp.where(lane == 0, 0.0, shift_lanes(here, 1))
                beside = beside + jnp.where(row == ROWS - 1, 0.0, shift_rows(here, -1))
                beside = beside + jnp.where(row == 0, 0.0, shift_rows(here, 1))
                if x > 0:
                    beside = beside + state[tile(field, x - 1), :]
                if x < PLANES - 1:
                    beside = beside + state[tile(field, x + 1), :]
                total = c * (6.0 * here - beside) + jnp.tanh(here)
                for w in range(VARS):
                    total = total + mix[v][w] * values[w]
                for j in range(HERE):
                    if j != i:
                        total = total + OWN[i][j] * state[tile(j * VARS + v, x), :]
                partial[tile(field, x), :] = forcing[tile(field, x), :] - total


def damping(coef_sum, count):
    inverse = jnp.where(count > 0.0, 1.0 / jnp.maximum(count, 1.0), 0.0)
    coef_c = coef_sum * inverse
    return inverse, coef_c, 0.6 / (6.0 * coef_c + 2.0)


def rows_kernel(partial, yb, ya, other, coef, s_in, halves, s_win, edge, coefs):
    even_y = even_index("sy")
    peer = 1 - lax.axis_index("hb")
    for x in range(PLANES):
        for i in range(HERE):
            for v in range(VARS):
                total = partial[tile(i * VARS + v, x), :]
                for j in range(HERE):
                    total = total - OTHER[i][j] * other[peer, tile(j * VARS + v, x), :]
                for half in range(2):
                    halves[half, tile(i * VARS + v, x), :] = total[:, half * 128 : (half + 1) * 128]
    count = FIELDS * PLANES
    for half in range(2):
        lanes = pl.ds(half * 128, 128)
        coefs[half] = coef[:, lanes]
        at_a, at_b = (ya[pl.ds(0, count), lanes], yb[pl.ds(0, count), lanes])
        for y, halo in ((0, choose(even_y, at_b, at_a)), (ROWS - 1, choose(even_y, at_a, at_b))):
            c4 = coefs[half, pl.ds(y, PLANES, stride=ROWS), :]
            edge[pl.ds(0, PLANES), :] = c4
            edge[pl.ds(PLANES, PLANES), :] = c4
            c8 = edge[...]
            c60 = jnp.concatenate([c8] * (count // 8) + [c8[: count % 8]], axis=0)
            rows = pl.ds(y, count, stride=ROWS)
            halves[half, rows, :] = halves[half, rows, :] + c60 * halo
    s_win[...] = s_in[...]
    for half, (above, below) in enumerate(((6, 1), (5, 2))):
        lanes = pl.ds(half * 128, 128)
        at_a, at_b = (ya[pl.ds(64, WIN), lanes], yb[pl.ds(64, WIN), lanes])
        s_win[row_of(below), :] = s_win[row_of(below), :] + choose(even_y, at_b, at_a)
        s_win[row_of(above), :] = s_win[row_of(above), :] + choose(even_y, at_a, at_b)


def outer_kernel(
    partial, xb, xa, coef, agg, s_win, mb, ma, residual, r_win, sums, rims, summed, scaled
):
    even_x, even_y = (even_index("sx"), even_index("sy"))
    for x in range(PLANES):
        c = coef[pl.ds(x * ROWS, ROWS), :]
        for field in range(FIELDS):
            face = pl.ds(field * ROWS, ROWS)
            total = jnp.concatenate([partial[h, tile(field, x), :] for h in range(2)], axis=1)
            if x == 0:
                total = total + c * choose(even_x, xb[face, :], xa[face, :])
            if x == PLANES - 1:
                total = total + c * choose(even_x, xa[face, :], xb[face, :])
            residual[tile(field, x), :] = total
    restrict(residual, lambda x: jnp.ones((ROWS, NZ), F32), agg, r_win, sums, rims, summed)
    for p in range(2):
        _, _, scale = damping(s_win[window(p, FIELDS), :], r_win[window(p, FIELDS), :])
        for field in range(GROUP):
            scaled[window(p, field), :] = scale * r_win[window(p, field), :]
    pieces = ((scaled, 4, 3), (r_win, 5, 2), (r_win, 6, 1))
    for n, (ref, above, below) in enumerate(pieces):
        high, low = (ref[row_of(above), :], ref[row_of(below), :])
        ma[pl.ds(n * WIN, WIN), :] = choose(even_y, high, low)
        mb[pl.ds(n * WIN, WIN), :] = choose(even_y, low, high)


def store_kernel(values, r_in, out, r_out, sems):
    copy = pltpu.make_async_copy(values, out, sems.at[0])
    copy.start()
    r_out[...] = r_in[...]
    copy.wait()


EDGE_ROWS = 6


def first_kernel(r_in, s_win, mb, ma, xb, xa, delta, r_win):
    even_x, even_y = (even_index("sx"), even_index("sy"))
    r_win[...] = r_in[...]
    pieces = []
    for n in range(3):
        at_a, at_b = (ma[pl.ds(n * WIN, WIN), :], mb[pl.ds(n * WIN, WIN), :])
        pieces.append((choose(even_y, at_b, at_a), choose(even_y, at_a, at_b)))
    for n, below, above in ((1, 1, 6), (2, 2, 5)):
        r_win[row_of(below), :] = r_win[row_of(below), :] + pieces[n][0]
        r_win[row_of(above), :] = r_win[row_of(above), :] + pieces[n][1]
    for p in range(2):
        _, _, scale = damping(s_win[window(p, FIELDS), :], r_win[window(p, FIELDS), :])
        for field in range(GROUP):
            delta[window(p, field), :] = scale * r_win[window(p, field), :]
    delta[row_of(0), :] = pieces[0][0]
    delta[row_of(7), :] = pieces[0][1]
    for r in range(EDGE_ROWS):
        low = delta[pl.ds(r + 1, GROUP, stride=ROWS), :]
        high = delta[pl.ds(GROUP * ROWS + r + 1, GROUP, stride=ROWS), :]
        xa[pl.ds(r * GROUP, GROUP), :] = choose(even_x, high, low)
        xb[pl.ds(r * GROUP, GROUP), :] = choose(even_x, low, high)


def second_kernel(mixing, r_win, s_win, delta, partial):
    lane = iota((ROWS, CZ), 1)
    mix = spread(mixing, CZ)
    for p in range(2):
        inverse, coef_c, scale = damping(s_win[window(p, FIELDS), :], r_win[window(p, FIELDS), :])
        for i in range(HERE):
            values = [delta[window(p, i * VARS + v), :] for v in range(VARS)]
            for v in range(VARS):
                field = i * VARS + v
                here = values[v]
                beside = jnp.where(lane == CZ - 1, 0.0, shift_lanes(here, -1))
                beside = beside + jnp.where(lane == 0, 0.0, shift_lanes(here, 1))
                beside = beside + shift_rows(here, -1) + shift_rows(here, 1)
                beside = beside + delta[window(1 - p, field), :]
                total = coef_c * (6.0 * here - beside)
                start = s_win[window(p, field), :] * inverse
                total = total + (jnp.tanh(start + here) - jnp.tanh(start))
                for w in range(VARS):
                    total = total + mix[v][w] * values[w]
                for j in range(HERE):
                    if j != i:
                        total = total + OWN[i][j] * delta[window(p, j * VARS + v), :]
                partial[window(p, field), :] = here + scale * (r_win[window(p, field), :] - total)
        partial[window(p, FIELDS), :] = coef_c


def final_kernel(
    partial, xb, xa, other, state, agg, corrected, change, fine, own, beside, halos, result, sems
):
    even_x = even_index("sx")
    peer = 1 - lax.axis_index("hb")
    for r in range(EDGE_ROWS):
        at_a, at_b = (xa[pl.ds(r * GROUP, GROUP), :], xb[pl.ds(r * GROUP, GROUP), :])
        rows = pl.ds(r + 1, GROUP, stride=ROWS)
        halos[0, rows, :] = choose(even_x, at_b, at_a)
        halos[1, rows, :] = choose(even_x, at_a, at_b)
    for p in range(2):
        for r in (0, ROWS - 1):
            halos[p, pl.ds(r, GROUP, stride=ROWS), :] = jnp.zeros((GROUP, CZ), F32)
    for p in range(2):
        coef_c = partial[window(p, FIELDS), :]
        scale = 0.6 / (6.0 * coef_c + 2.0)
        for i in range(HERE):
            for v in range(VARS):
                field = i * VARS + v
                total = coef_c * halos[p, pl.ds(field * ROWS, ROWS), :]
                for j in range(HERE):
                    total = total - OTHER[i][j] * other[peer, window(p, j * VARS + v), :]
                change[window(p, field), :] = partial[window(p, field), :] + scale * total
        change[window(p, FIELDS), :] = jnp.zeros((ROWS, CZ), F32)
    twice = (iota((CZ, NZ), 1) >> 1 == iota((CZ, NZ), 0)).astype(BF16)
    for half in range(2):
        fine[half] = pair_sums(change[...], twice[:, half * 128 : (half + 1) * 128])
    for half in range(2):
        rows = [fine[half, row_of(b + 1), :] for b in range(6)]
        for b in range(4):
            own[half, row_of(2 * b), :] = rows[b + 1]
            own[half, row_of(2 * b + 1), :] = rows[b + 1]
            beside[half, row_of(2 * b), :] = rows[b]
            beside[half, row_of(2 * b + 1), :] = rows[b + 2]
    masks = [moved_mask(agg, p) > 0.0 for p in range(2)]
    copies = []
    for i in range(HERE):
        for field in range(i * VARS, (i + 1) * VARS):
            for p in range(2):
                for half in range(2):
                    lanes = pl.ds(half * 128, 128)
                    moved = masks[p][:, half * 128 : (half + 1) * 128]
                    kept = own[half, window(p, field), :]
                    went = beside[half, window(p, field), :]
                    even, odd = (tile(field, 2 * p), tile(field, 2 * p + 1))
                    result[even, lanes] = state[even, lanes] + kept
                    result[odd, lanes] = state[odd, lanes] + jnp.where(moved, went, kept)
        rows = pl.ds(i * VARS * PLANES * ROWS, VARS * PLANES * ROWS)
        copies.append(pltpu.make_async_copy(result.at[rows, :], corrected.at[rows, :], sems.at[i]))
        copies[-1].start()
    for copy in copies:
        copy.wait()


VMEM = pl.BlockSpec(memory_space=pltpu.VMEM)
HBM = pl.BlockSpec(memory_space=pltpu.HBM)


def call(kernel, outs, scratch, *args, spaces=(), out_space=VMEM, sems=0):
    spaces = list(spaces) + [VMEM] * (len(args) - len(spaces))
    args = [
        pltpu.with_memory_space_constraint(a, pltpu.HBM) if s is HBM else a
        for a, s in zip(args, spaces)
    ]
    outs = [o if hasattr(o, "dtype") else jax.ShapeDtypeStruct(o, F32) for o in outs]
    return pl.pallas_call(
        kernel,
        out_shape=outs,
        in_specs=spaces,
        out_specs=out_space if isinstance(out_space, list) else [out_space] * len(outs),
        scratch_shapes=[pltpu.VMEM(s, F32) for s in scratch]
        + ([pltpu.SemaphoreType.DMA((sems,))] if sems else []),
        compiler_params=pltpu.CompilerParams(vmem_limit_bytes=40 * 1024 * 1024),
        name=kernel.__name__,
    )(*args)


def swap_pairs(axis, first):
    size = lax.axis_size(axis)
    up = [(i, i + 1) for i in range(first, size - 1, 2)]
    return up + [(j, i) for i, j in up]


def shards(state, forcing, coef, mixing, agglomerate):
    shape = state.shape
    fine = (FIELDS * PLANES * ROWS, NZ)
    wins = (WIN * ROWS, CZ)
    state = state.reshape(fine)
    forcing = forcing.reshape(fine)
    coef = coef.reshape(PLANES * ROWS, NZ)
    agg = agglomerate.reshape(PLANES * ROWS, NZ)

    def swap(value, axis, first=0):
        return lax.ppermute(value, axis, swap_pairs(axis, first))

    halves = (2, FIELDS * PLANES * ROWS, 128)
    sums = (WIN * ROWS, NZ)
    rims = (2, WIN * ROWS, 128)
    x_face = (FIELDS * ROWS, NZ)
    y_face = (64 + WIN, NZ)
    yb, xb, xa, ya, state, forcing, coef, agg, s_win = call(
        edges_kernel,
        [y_face, x_face, x_face, y_face, fine, fine, coef.shape, agg, wins],
        [halves, sums, rims, wins],
        state, forcing, coef, agg,
        spaces=[HBM] * 4,
        sems=4,
    )
    yb = swap(yb, "sy", 1)
    xb = swap(xb, "sx", 1)
    xa = swap(xa, "sx")
    ya = swap(ya, "sy")
    other = lax.all_gather(state, "hb")
    (partial,) = call(inner_kernel, [fine], [], mixing, state, forcing, coef)
    msg = (3 * WIN, CZ)
    partial, s_win = call(
        rows_kernel,
        [halves, wins],
        [(8, 128), (2, PLANES * ROWS, 128)],
        partial, yb, ya, other, coef, s_win,
    )
    mb, ma, residual, r_win = call(
        outer_kernel,
        [msg, msg, fine, wins],
        [sums, rims, wins, wins],
        partial, xb, xa, coef, agg, s_win,
    )
    mb = swap(mb, "sy", 1)
    ma = swap(ma, "sy")
    residual, r_win = call(
        store_kernel, [fine, wins], [], residual, r_win, out_space=[HBM, VMEM], sems=1
    )
    face = (EDGE_ROWS * GROUP, CZ)
    db, da, delta, r_win = call(
        first_kernel, [face, face, wins, wins], [], r_win, s_win, mb, ma
    )
    db = swap(db, "sx", 1)
    da = swap(da, "sx")
    other_delta = lax.all_gather(delta, "hb")
    (step,) = call(second_kernel, [wins], [], mixing, r_win, s_win, delta)
    (corrected,) = call(
        final_kernel,
        [fine],
        [wins, (2,) + wins, (2,) + wins, (2,) + wins, (2, GROUP * ROWS, CZ), fine],
        step, db, da, other_delta, state, agg,
        out_space=HBM,
        sems=HERE,
    )
    return corrected.reshape(shape), residual.reshape(shape)


def solution(mesh):
    whole = P("hb", None, "sx", "sy", None)
    return jax.shard_map(
        shards,
        mesh=mesh,
        in_specs=(whole, whole, P("sx", "sy", None), P(), P("sx", "sy", None)),
        out_specs=(whole, whole),
        check_vma=False,
    )
```
